128 devices in a mesh: req: 4 (over x_lo, core), head: 32 (over z, y, x_hi).
Axes of the slice: x: 4 (x_hi: 2, x_lo: 2; x = x_hi * 2 + x_lo), y: 4, z: 4, core: 2. Of those that a mesh axis runs over, the one named last changes fastest.
Arguments:
- x_input: bfloat16 [8, 512, 16384], P('req', None, 'head'), may hold values from -6 to 6
- z_gate: bfloat16 [8, 512, 16384], P('req', None, 'head'), may hold values from -6 to 6
- bc_input: bfloat16 [8, 512, 4096], P('req'), may hold values from -6 to 6
- dt_raw: float32 [8, 256, 512], P('req', 'head'), may hold values from -7 to 1.25
- a_log: float32 [256], P('head'), may hold values from -3 to 1.26
- d_skip: float32 [256], P('head'), may hold values from 0.5 to 2
- conv_x: bfloat16 [4, 16384], P(None, 'head'), may hold values from -3 to 3
- conv_bc: bfloat16 [4, 4096], replicated, may hold values from -3 to 3
- out_weight: bfloat16 [16384, 8192], P('head'), may hold values from -0.046875 to 0.046875
- pool_state: float32 [16, 16384, 256], P('req', 'head'), may hold values from -1.75 to 1.75
- pool_xtail: bfloat16 [16, 3, 16384], P('req', None, 'head'), may hold values from -6 to 6
- pool_bctail: bfloat16 [16, 3, 4096], P('req'), may hold values from -6 to 6
- pool_dev: int32 [8, 1], replicated, may hold values from 0 to 3; in each aligned block of 2 rows (0 to 1, 2 to 3, ...) at most 2 rows name the same one
- pool_slot: int32 [8], replicated, may hold values from 0 to 3
- lengths: int32 [8], P('req'), may hold values from 128 to 512, as said below
Outputs:
- mixed: float32 [8, 512, 8192], P('req', 'head')
- final_state: float32 [8, 16384, 256], P('req', 'head')
The draws below stay inside these ranges and needn't reach their ends.
Inputs may be any that keep to these rules, and one draw needn't show every extreme that they name: pool_dev[r, 0] is the pool shard, an index of req, that holds request r's cached prefix; among the 2 requests of one request group no shard is named by more than 2 requests, and in some group one shard is named by exactly 2. `lengths`: in every draw the longest suffix has exactly 512 positions and the shortest exactly 128.
All inputs are finite; a program needn't handle non-finite values.
Results may differ from the reference program's by a relative error of at most 0.0039.
Values sent between devices are 32-bit elements; how exact they have to be, the bound alone decides.
No kernel may reach another device: no remote copies, remote signals or barrier semaphores. Data moves between devices by JAX's collectives and lax.ppermute only.
A program may use at most 128 MiB of HBM per device.

```python
import math
import jax
import jax.numpy as jnp
import numpy as np
from jax import lax

D = 8192
HEADS = 256
HEADDIM = 64
STATE = 256
GROUPS = 8
CONV = 4
BLOCK = 128
SUFFIX_LIMIT = 512
REQ_DEV = 2
SLOTS = 4
MINLEN = 128
INNER = 16384
BCW = 4096
REQUEST_TOTAL = 8
POOL = 16
CAP = 2
N_REQ = 4


def draw_a_log(key, part):
    key = jax.random.fold_in(key, 17)
    upper_end = math.log(3.5)
    return jax.random.uniform(key, (HEADS,), jnp.float32, math.log(0.05), upper_end)


def draw_dt_raw(key, part):
    key = jax.random.fold_in(key, 29)
    height_random_key, spurt_random_key = jax.random.split(key)
    lower_end = 4.0
    upper_end = 9.0
    minimum_step = jnp.exp(jax.random.uniform(height_random_key, (REQUEST_TOTAL, HEADS, SUFFIX_LIMIT), jnp.float32, math.log(lower_end), math.log(upper_end))) / SUFFIX_LIMIT
    spurt_mask = jax.random.uniform(spurt_random_key, (REQUEST_TOTAL, 1, SUFFIX_LIMIT), jnp.float32) < 2.0 / SUFFIX_LIMIT
    step_length = jnp.where(spurt_mask, 1.5, minimum_step)
    return jnp.log(jnp.expm1(step_length))


def draw_lengths(key, part):
    key = jax.random.fold_in(key, 41)
    value_key, long_key, short_key = jax.random.split(key, 3)
    drawn_len = jax.random.randint(value_key, (REQUEST_TOTAL,), MINLEN, SUFFIX_LIMIT + 1)
    longest = jax.random.randint(long_key, (), 0, REQUEST_TOTAL)
    shortest = (longest + jax.random.randint(short_key, (), 1, REQUEST_TOTAL)) % REQUEST_TOTAL
    request_ids = jnp.arange(REQUEST_TOTAL)
    drawn_len = jnp.where(request_ids == longest, SUFFIX_LIMIT, drawn_len)
    return jnp.where(request_ids == shortest, MINLEN, drawn_len).astype(jnp.int32)


def touch_ends(drawn, rng, least, top_value):
    longest = drawn.shape.index(max(drawn.shape))
    spots = []
    for shift in (0, 1):
        where = [jax.random.randint(jax.random.fold_in(rng, axis), (), 0, length) for axis, length in enumerate(drawn.shape)]
        where[longest] = (where[longest] + shift) % drawn.shape[longest]
        spots.append(tuple(where))
    return drawn.at[spots[0]].set(least).at[spots[1]].set(top_value)


def with_spikes(result, rng, source, target, shards_of, factor):
    owner, partner = [(jnp.arange(result.shape[position]) // (result.shape[position] // shards_of)).reshape([-1 if axis == position else 1 for axis in range(result.ndim)]) for position in (source, target)]
    chosen = jax.random.permutation(rng, shards_of)[partner]
    strong = (owner == chosen) | (owner == (partner + shards_of // 2) % shards_of)
    return jnp.where(strong, factor * result, result)


def level_of(stream_key, extent, cuts, least, largest):
    level, own = 1.0, jax.random.fold_in(stream_key, 6)
    for dim, shards_of in cuts:
        steps = jnp.exp(jax.random.uniform(jax.random.fold_in(own, dim), (shards_of,), jnp.float32, least / len(cuts), largest / len(cuts)))
        level = level * jnp.repeat(steps, extent[dim] // shards_of).reshape([-1 if axis == dim else 1 for axis in range(len(extent))])
    return level


def deal_out(stream_key, own, number, rows, count, top, limit, lean):
    order = jax.random.permutation(stream_key, count)
    packed, ordinary = shares(count, rows * top, limit, lean, True), shares(count, rows * top, limit, lean, False)
    places = jnp.arange(count)

    def named(sizes, offset_by):
        used = int((sizes > 0).sum())
        fixed = max(1, used // 4)
        passed = fixed + (places - fixed + offset_by * (used - fixed)) % max(1, count - fixed)
        return jnp.zeros((count,), jnp.int32).at[order[jnp.where(places < fixed, places, passed)]].set(jnp.asarray(sizes, jnp.int32))

    sizes = jnp.where(number % 4 == 0, named(packed, number // 4), named(ordinary, number - number // 4 - 1))
    mixed = jax.random.permutation(jax.random.fold_in(own, 3), count)
    donor, receiver = mixed[0:count // 2 * 2:2], mixed[1:count // 2 * 2:2]
    room = jnp.minimum(sizes[donor] - 1, limit - sizes[receiver]) // 2
    room = jnp.where((donor == order[0]) | (receiver == order[0]) | (sizes[receiver] == 0), 0, jnp.maximum(room, 0))
    passed = jax.random.randint(jax.random.fold_in(own, 4), (count // 2,), 0, 1 << 20) % (room + 1)
    sizes = sizes.at[donor].add(-passed).at[receiver].add(passed)
    members = jnp.searchsorted(jnp.cumsum(sizes), jnp.arange(rows * top), side="right").astype(jnp.int32)
    listing = members.reshape(top, rows).T
    listing = listing[jax.random.permutation(jax.random.fold_in(own, 1), rows)]
    offset_by = jax.random.randint(jax.random.fold_in(own, 2), (rows, 1), 0, top)
    return jnp.take_along_axis(listing, (jnp.arange(top)[None, :] + offset_by) % top, axis=1)


def shares(count, total, bound, lean, full):
    portions = [(1 << 20) // math.isqrt(standing ** lean) + 1 for standing in range(1, count + 1)]
    largest = bound if full else min(bound, max(-(-total // count), total * portions[0] // sum(portions)))
    least = 1 if total - largest >= count - 1 else 0
    counts, rest = [largest] + [least] * (count - 1), total - largest - least * (count - 1)
    while rest > 0:
        free = [i for i in range(1, count) if counts[i] < largest] or [i for i in range(1, count) if counts[i] < bound]
        pool, remaining = sum([portions[i] for i in free]), rest
        for i in free:
            extra = min(bound - counts[i], max(1, remaining * portions[i] // pool), rest)
            counts[i] = counts[i] + extra
            rest = rest - extra
    return np.array(counts)


def bell_draw(own_key, dims, spread, limit, cuts=(), kind=jnp.bfloat16):
    level = level_of(own_key, dims, cuts, -0.22, 0.18) if cuts else 1.0
    result = jax.random.normal(own_key, dims, jnp.float32) * spread * level
    return jnp.minimum(jnp.maximum(result, -limit), limit).astype(kind)


def heavy_noise(own_key, shape, spread, bound, cuts, heavy, held_as=jnp.bfloat16):
    result = spread * jax.random.normal(own_key, shape, jnp.float32)
    if cuts:
        result = result * level_of(own_key, shape, cuts, -0.22, 0.18)
    return jnp.clip(with_spikes(result, jax.random.fold_in(own_key, 3), *heavy), -bound, bound).astype(held_as)


def setup_inputs(seed: int = 0) -> dict:
    arg_keys = jax.random.split(jax.random.key(seed), 16)
    x_input = bell_draw(arg_keys[0], (REQUEST_TOTAL, SUFFIX_LIMIT, INNER), 1.0, 6.0, ((0, 4), (2, 32)))
    z_gate = heavy_noise(arg_keys[1], (REQUEST_TOTAL, SUFFIX_LIMIT, INNER), 1.0, 6.0, ((0, 4), (2, 32)), (2, 1, 32, 2.75))
    bc_input = bell_draw(arg_keys[2], (REQUEST_TOTAL, SUFFIX_LIMIT, BCW), 1.0, 6.0, ((0, 4),))
    dt_raw = draw_dt_raw(jax.random.fold_in(arg_keys[15], 71), 0)
    a_log = draw_a_log(jax.random.fold_in(arg_keys[15], 71), 0)
    d_skip = jnp.clip(0.5 + 1.5 * jax.random.uniform(arg_keys[5], (HEADS,), jnp.float32) ** level_of(arg_keys[5], (HEADS,), ((0, 32),), -0.2, 0.2), 0.5, 2.0)
    conv_x = bell_draw(arg_keys[6], (CONV, INNER), CONV ** -0.5, 3.0, ((1, 32),))
    conv_bc = bell_draw(arg_keys[7], (CONV, BCW), CONV ** -0.5, 3.0)
    out_weight = bell_draw(arg_keys[8], (INNER, D), INNER ** -0.5, 0.046875, ((0, 32),))
    pool_state = bell_draw(arg_keys[9], (POOL, INNER, STATE), 0.3, 1.75, ((0, 4), (1, 32)), jnp.float32)
    pool_xtail = bell_draw(arg_keys[10], (POOL, CONV - 1, INNER), 1.0, 6.0, ((0, 4), (2, 32)))
    pool_bctail = bell_draw(arg_keys[11], (POOL, CONV - 1, BCW), 1.0, 6.0, ((0, 4),))
    pool_dev_keys = jax.random.split(jax.random.fold_in(arg_keys[12], 1), REQUEST_TOTAL // REQ_DEV)
    pool_dev_turns = jax.random.permutation(jax.random.fold_in(arg_keys[12], 3), REQUEST_TOTAL // REQ_DEV)
    pool_dev = jax.vmap(lambda own, number: deal_out(jax.random.fold_in(arg_keys[12], 2), own, number, REQ_DEV, N_REQ, 1, CAP, 2))(pool_dev_keys, pool_dev_turns).reshape((REQUEST_TOTAL, 1))
    pool_slot = touch_ends(jax.random.randint(arg_keys[13], (REQUEST_TOTAL,), 0, SLOTS), jax.random.fold_in(arg_keys[13], 1), 0, SLOTS - 1).astype(jnp.int32)
    lengths = draw_lengths(jax.random.fold_in(arg_keys[15], 71), 0)
    return dict(x_input=x_input, z_gate=z_gate, bc_input=bc_input, dt_raw=dt_raw, a_log=a_log, d_skip=d_skip, conv_x=conv_x, conv_bc=conv_bc, out_weight=out_weight, pool_state=pool_state, pool_xtail=pool_xtail, pool_bctail=pool_bctail, pool_dev=pool_dev, pool_slot=pool_slot, lengths=lengths)


def conv_silu(prefix_rows, sequence, kernel):
    window = jnp.concatenate([prefix_rows, sequence], axis=-2).astype(jnp.float32)
    length = sequence.shape[-2]
    accumulated = jnp.zeros(sequence.shape, jnp.float32)
    for offset in range(kernel.shape[0]):
        accumulated = accumulated + window[..., offset:offset + length, :] * kernel[offset].astype(jnp.float32)
    return jax.nn.silu(accumulated).astype(jnp.bfloat16)


def block_scan(values, b_rows, c_rows, time_step, decay_rate, d_skip, initial):
    length, head_count, head_width = values.shape
    state_size = b_rows.shape[1]
    blocks = length // BLOCK
    inputs = values.astype(jnp.float32).reshape(blocks, BLOCK, head_count, head_width)
    b_block = b_rows.astype(jnp.float32).reshape(blocks, BLOCK, state_size)
    c_block = c_rows.astype(jnp.float32).reshape(blocks, BLOCK, state_size)
    step_block = time_step.reshape(head_count, blocks, BLOCK)
    decay_log = jnp.cumsum(-decay_rate[:, None, None] * step_block, axis=2)
    scores = jnp.einsum("cin,cjn->cij", c_block, b_block, precision=lax.Precision.HIGHEST)
    causal = jnp.arange(BLOCK)[:, None] >= jnp.arange(BLOCK)[None, :]
    log_gap = jnp.where(causal, decay_log[:, :, :, None] - decay_log[:, :, None, :], 0.0)
    mixing = jnp.where(causal, jnp.exp(log_gap), 0.0) * scores[None] * step_block[:, :, None, :]
    within = jnp.einsum("hcij,cjhp->cihp", mixing, inputs, precision=lax.Precision.HIGHEST)
    weight_in = jnp.transpose(jnp.exp(decay_log[:, :, -1:] - decay_log) * step_block, (1, 2, 0))
    block_state = jnp.einsum("cjhp,cjn->chpn", inputs * weight_in[:, :, :, None], b_block, precision=lax.Precision.HIGHEST)
    factor = jnp.transpose(jnp.exp(decay_log[:, :, -1]))

    def advance(running, pieces):
        shrink, addend = pieces
        return shrink[:, None, None] * running + addend, running

    closing, entering = lax.scan(advance, initial, (factor, block_state))
    carried = jnp.einsum("cin,chpn->cihp", c_block, entering, precision=lax.Precision.HIGHEST)
    carried = carried * jnp.exp(jnp.transpose(decay_log, (1, 2, 0)))[:, :, :, None]
    output = within + carried + d_skip[None, None, :, None] * inputs
    return output.reshape(length, head_count, head_width), closing


def reference(x_input, z_gate, bc_input, dt_raw, a_log, d_skip, conv_x, conv_bc, out_weight, pool_state, pool_xtail, pool_bctail, pool_dev, pool_slot, lengths):
    decay_rate = jnp.exp(a_log)
    per_group = HEADS // GROUPS
    positions = jnp.arange(SUFFIX_LIMIT)

    def one_request(request):
        entry_row = (pool_dev[request, 0] * SLOTS + pool_slot[request]).astype(jnp.int32)
        initial = pool_state[entry_row].reshape(GROUPS, per_group, HEADDIM, STATE)
        x_conv = conv_silu(pool_xtail[entry_row], x_input[request], conv_x)
        bc_conv = conv_silu(pool_bctail[entry_row], bc_input[request], conv_bc)
        live_mask = (positions < lengths[request]).astype(jnp.float32)
        time_step = jax.nn.softplus(dt_raw[request]) * live_mask[None, :]
        grouped_x = jnp.transpose(x_conv.reshape(SUFFIX_LIMIT, GROUPS, per_group, HEADDIM), (1, 0, 2, 3))
        b_groups = jnp.transpose(bc_conv[:, :GROUPS * STATE].reshape(SUFFIX_LIMIT, GROUPS, STATE), (1, 0, 2))
        c_groups = jnp.transpose(bc_conv[:, GROUPS * STATE:].reshape(SUFFIX_LIMIT, GROUPS, STATE), (1, 0, 2))
        outputs, closing = lax.map(
            lambda pieces: block_scan(*pieces),
            (grouped_x, b_groups, c_groups, time_step.reshape(GROUPS, per_group, SUFFIX_LIMIT),
             decay_rate.reshape(GROUPS, per_group), d_skip.reshape(GROUPS, per_group), initial))
        mixed_y = jnp.transpose(outputs, (1, 0, 2, 3)).reshape(SUFFIX_LIMIT, INNER)
        gated_rows = (mixed_y * jax.nn.silu(z_gate[request].astype(jnp.float32)) * live_mask[:, None]).astype(jnp.bfloat16)
        accumulated = jnp.dot(gated_rows, out_weight, preferred_element_type=jnp.float32)
        return accumulated, closing.reshape(INNER, STATE)

    mixed_out, final_state = lax.map(one_request, jnp.arange(REQUEST_TOTAL).astype(jnp.int32))
    return (mixed_out, final_state)
```

```python
import jax
import jax.numpy as jnp
from jax import lax
from jax.experimental import pallas as pl
from jax.experimental.pallas import tpu as pltpu
from jax.sharding import PartitionSpec as P

HEADS = 256
STATE = 256
GROUPS = 8
BLOCK = 128
AXES = ("req", "head")
MIB = 1 << 20


def partner(z=0, y=0, hi=0, lo=0, core=0):
    pairs = []
    for source in range(128):
        pairs.append((source, source ^ (lo << 6 | core << 5 | z << 3 | y << 1 | hi)))
    return pairs


def swap(array, **bits):
    return lax.ppermute(array, AXES, partner(**bits))


def flip_if(bit, array, axis):
    return jnp.where(bit == 1, jnp.flip(array, axis), array)


def from_root(value, axis, source):
    kept = jnp.where(lax.axis_index(axis) == source, value, 0).astype(value.dtype)
    return lax.psum(kept, axis)


def conv_silu(prefix_rows, sequence, kernel):
    window = jnp.concatenate([prefix_rows, sequence.astype(jnp.float32)], axis=-2)
    length = sequence.shape[-2]
    accumulated = jnp.zeros(sequence.shape, jnp.float32)
    for offset in range(kernel.shape[0]):
        accumulated = accumulated + window[..., offset : offset + length, :] * kernel[
            offset
        ].astype(jnp.float32)
    return jax.nn.silu(accumulated).astype(jnp.bfloat16)


def block_scan(values, b_rows, c_rows, time_step, decay_rate, d_skip, initial):
    length, head_count, head_width = values.shape
    state_size = b_rows.shape[1]
    blocks = length // BLOCK
    inputs = values.astype(jnp.float32).reshape(blocks, BLOCK, head_count, head_width)
    b_narrow = b_rows.reshape(blocks, BLOCK, state_size)
    c_narrow = c_rows.reshape(blocks, BLOCK, state_size)
    b_block = b_narrow.astype(jnp.float32)
    c_block = c_narrow.astype(jnp.float32)
    step_block = time_step.reshape(head_count, blocks, BLOCK)
    decay_log = jnp.cumsum(-decay_rate[:, None, None] * step_block, axis=2)
    scores = jnp.einsum("cin,cjn->cij", c_narrow, b_narrow, preferred_element_type=jnp.float32)
    causal = jnp.arange(BLOCK)[:, None] >= jnp.arange(BLOCK)[None, :]
    log_gap = jnp.where(causal, decay_log[:, :, :, None] - decay_log[:, :, None, :], 0.0)
    mixing = jnp.where(causal, jnp.exp(log_gap), 0.0) * scores[None] * step_block[:, :, None, :]
    within = jnp.einsum("hcij,cjhp->cihp", mixing, inputs, precision=lax.Precision.HIGHEST)
    weight_in = jnp.transpose(jnp.exp(decay_log[:, :, -1:] - decay_log) * step_block, (1, 2, 0))
    block_state = jnp.einsum(
        "cjhp,cjn->chpn",
        inputs * weight_in[:, :, :, None],
        b_block,
        precision=lax.Precision.HIGHEST,
    )
    factor = jnp.transpose(jnp.exp(decay_log[:, :, -1]))

    def advance(running, pieces):
        shrink, addend = pieces
        return (shrink[:, None, None] * running + addend, running)

    closing, entering = lax.scan(advance, initial, (factor, block_state))
    carried = jnp.einsum("cin,chpn->cihp", c_block, entering, precision=lax.Precision.HIGHEST)
    carried = carried * jnp.exp(jnp.transpose(decay_log, (1, 2, 0)))[:, :, :, None]
    output = within + carried + d_skip[None, None, :, None] * inputs
    return (output.reshape(length, head_count, head_width), closing)


def own_group(array, group_index):
    b_part = lax.dynamic_slice_in_dim(array, group_index * STATE, STATE, array.ndim - 1)
    c_part = lax.dynamic_slice_in_dim(array, (GROUPS + group_index) * STATE, STATE, array.ndim - 1)
    return jnp.concatenate([b_part, c_part], axis=-1)


ORDER = ((2, 1, 0, 3), (2, 3, 0, 1))
TILE = 512
ROWS = 16


def product_kernel(own, near, far, cross_low, cross_high, w_own, w_far, *outs):
    own_side = jnp.concatenate([own[...], near[...]], axis=0).astype(jnp.bfloat16)
    far_side = jnp.concatenate([cross_low[...], cross_high[...], far[...]], axis=0).astype(
        jnp.bfloat16
    )
    total = jnp.dot(own_side, w_own[...], preferred_element_type=jnp.float32)
    total += jnp.dot(far_side, w_far[...].astype(jnp.bfloat16), preferred_element_type=jnp.float32)

    def emit(major_is_y):
        def piece(major, side):
            rows = []
            for minor in ORDER[side]:
                z, y = (minor, major) if major_is_y else (major, minor)
                start = side * 16 * ROWS + (z * 4 + y) * ROWS
                rows.append(total[start : start + ROWS])
            return rows

        first, third, one_b, three_a, zero_a, zero_b = outs

        def put(ref, rows):
            for at, block in enumerate(rows):
                ref[at * ROWS : (at + 1) * ROWS, :] = block

        put(first, piece(2, 0) + piece(1, 0))
        put(third, piece(2, 1) + piece(3, 1))
        put(one_b, piece(1, 1))
        put(three_a, piece(3, 0))
        put(zero_a, piece(0, 0))
        put(zero_b, piece(0, 1))

    return emit


def product(blocks, w_own, w_far, y_first):
    width = w_own.shape[1]
    depth = w_own.shape[0]

    def kernel(*refs):
        product_kernel(*refs)(y_first)

    lines = 4 * ROWS
    heights = (2 * lines, 2 * lines, lines, lines, lines, lines)
    return pl.pallas_call(
        kernel,
        grid=(width // TILE,),
        in_specs=[pl.BlockSpec(b.shape, lambda i: (0, 0)) for b in blocks]
        + [pl.BlockSpec((depth, TILE), lambda i: (0, i))] * 2,
        out_specs=[pl.BlockSpec((h, TILE), lambda i: (0, i)) for h in heights],
        out_shape=[jax.ShapeDtypeStruct((h, width), jnp.float32) for h in heights],
        compiler_params=pltpu.CompilerParams(vmem_limit_bytes=48 * MIB),
        cost_estimate=pl.CostEstimate(
            flops=2 * 512 * 2 * depth * width,
            bytes_accessed=4 * (4 * 256 * depth + 2 * depth * width + 512 * width),
            transcendentals=0,
        ),
    )(*blocks, w_own, w_far)


def exchange(parts, axis):
    first, third, one_b, three_a, zero_a, zero_b = parts
    lines = one_b.shape[0]
    got1 = swap(first, **{axis: 1})
    got3 = swap(third, **{axis: 3})
    back1 = swap(one_b + got3[:lines], **{axis: 1})
    back3 = swap(three_a + got1[:lines], **{axis: 3})
    return (zero_a + got1[lines:] + back3, zero_b + got3[lines:] + back1)


def next_parts(sums):
    a, b = sums
    line = a.shape[0] // 4
    return (
        a[: 2 * line],
        b[: 2 * line],
        b[3 * line :],
        a[3 * line :],
        a[2 * line : 3 * line],
        b[2 * line : 3 * line],
    )


def project(gated, out_weight, coords):
    z, y, hi, lo, core = coords
    place = 2 * hi + lo
    width = out_weight.shape[1] // 4
    half = width // 2
    pieces = [
        lax.dynamic_slice_in_dim(out_weight, place * width + c * half, half, 1)
        for c in (core, 1 - core)
    ]
    outgoing = lax.dynamic_slice_in_dim(out_weight, (3 - place) * width + core * half, half, 1)
    far_own = swap(outgoing.astype(jnp.float32), hi=1, lo=1)
    far_other = swap(far_own, core=1)
    w_far = (far_own, far_other)
    requests = gated.shape[0]
    mixed = []
    for request in range(requests):
        done = []
        for part in range(2):
            own = gated[request, :, :, part].reshape(16 * ROWS, -1)
            near = swap(own, lo=1)
            far = swap(own, hi=1, lo=1)
            cross_low = swap(far[: 8 * ROWS], lo=1)
            cross_high = swap(near[8 * ROWS :], hi=1, lo=1)
            blocks = (own, near, far, cross_low, cross_high)
            halves = []
            for c, axes in enumerate((("y", "z"), ("z", "y"))):
                sums = exchange(product(blocks, pieces[c], w_far[c], c == 0), axes[0])
                halves.append(exchange(next_parts(sums), axes[1]))
            done.append(halves)

        def pick(part, side):
            return jnp.stack([done[part][c][side] for c in range(2)])

        kept = [jnp.where(hi == 0, pick(0, side), pick(1, side)) for side in range(2)]
        away = [jnp.where(hi == 0, pick(1, side), pick(0, side)) for side in range(2)]
        got = jnp.stack(
            [kept[0], swap(kept[1], lo=1), swap(away[0], hi=1), swap(away[1], hi=1, lo=1)]
        ).reshape(2, 2, 2, ROWS, half)
        got = flip_if(core, flip_if(lo, flip_if(hi, got, 0), 1), 2)
        mixed.append(jnp.transpose(got, (3, 0, 1, 2, 4)).reshape(ROWS, 4 * width))
    return jnp.stack(mixed)


def on_device(
    x_input,
    z_gate,
    bc_input,
    dt_raw,
    a_log,
    d_skip,
    conv_x,
    conv_bc,
    out_weight,
    pool_state,
    pool_xtail,
    pool_bctail,
    pool_dev,
    pool_slot,
    lengths,
):
    req_count = lax.axis_size("req")
    my_req = lax.axis_index("req")
    my_head = lax.axis_index("head")
    coords = (my_head // 8, my_head // 2 % 4, my_head % 2, my_req // 2, my_req % 2)
    head_count = a_log.shape[0]
    requests = lengths.shape[0]
    length = x_input.shape[1]
    shard_width = x_input.shape[2]
    head_width = shard_width // head_count
    group_index = lax.axis_index("head") * head_count // (HEADS // GROUPS)
    tail_table = jnp.concatenate([pool_xtail, own_group(pool_bctail, group_index)], axis=-1).astype(
        jnp.float32
    )
    tail_shape = tail_table.shape[1:]
    hit_list = pool_dev[:, 0]
    state_cells = shard_width * STATE

    def fetch_one(request, carried):
        start_rows, tail_rows = carried
        slot_here = pool_slot[request]
        packed = jnp.concatenate(
            [
                lax.dynamic_index_in_dim(pool_state, slot_here, 0, keepdims=False).reshape(-1),
                lax.dynamic_index_in_dim(tail_table, slot_here, 0, keepdims=False).reshape(-1),
            ]
        )
        received = from_root(packed, "req", hit_list[request])
        local_row = request - my_req * requests
        owned_here = (local_row >= 0) & (local_row < requests)
        target = jnp.clip(local_row, 0, requests - 1)
        new_starts = lax.dynamic_update_index_in_dim(
            start_rows, received[:state_cells].reshape(shard_width, STATE), target, 0
        )
        new_tails = lax.dynamic_update_index_in_dim(
            tail_rows, received[state_cells:].reshape(tail_shape), target, 0
        )
        return (
            jnp.where(owned_here, new_starts, start_rows),
            jnp.where(owned_here, new_tails, tail_rows),
        )

    blank_rows = (
        jnp.zeros((requests, shard_width, STATE), jnp.float32),
        jnp.zeros((requests,) + tail_shape, jnp.float32),
    )
    start_rows, tail_rows = lax.fori_loop(0, req_count * requests, fetch_one, blank_rows)
    x_conv = conv_silu(tail_rows[:, :, :shard_width], x_input, conv_x)
    bc_conv = conv_silu(
        tail_rows[:, :, shard_width:],
        own_group(bc_input, group_index),
        own_group(conv_bc, group_index),
    )
    live_mask = (jnp.arange(length)[None, :] < lengths[:, None]).astype(jnp.float32)
    time_step = jax.nn.softplus(dt_raw) * live_mask[:, None, :]
    decay_rate = jnp.exp(a_log)
    head_x = x_conv.reshape(requests, length, head_count, head_width)
    initial = start_rows.reshape(requests, head_count, head_width, STATE)
    gate_rows = jax.nn.silu(z_gate.astype(jnp.float32)) * live_mask[:, :, None]
    scan_batch = jax.vmap(block_scan, in_axes=(0, 0, 0, 0, None, None, 0))
    outputs, closing = scan_batch(
        head_x, bc_conv[..., :STATE], bc_conv[..., STATE:], time_step, decay_rate, d_skip, initial
    )
    gated_rows = (outputs.reshape(requests, length, shard_width) * gate_rows).astype(jnp.bfloat16)
    relative = gated_rows.reshape(requests, 2, 2, 2, 2, 2, ROWS, shard_width)
    z, y = coords[:2]
    for axis, bit in ((1, z // 2), (2, z % 2), (3, y // 2), (4, y % 2)):
        relative = flip_if(bit, relative, axis)
    relative = relative.reshape(requests, 4, 4, 2, ROWS, shard_width).astype(jnp.float32)
    mixed_out = project(relative, out_weight, coords)
    final_state = closing.reshape(requests, shard_width, STATE)
    return (mixed_out, final_state)


def solution(mesh):
    return jax.shard_map(
        on_device,
        mesh=mesh,
        in_specs=(
            P("req", None, "head"),
            P("req", None, "head"),
            P("req", None, None),
            P("req", "head", None),
            P("head"),
            P("head"),
            P(None, "head"),
            P(),
            P("head", None),
            P("req", "head", None),
            P("req", None, "head"),
            P("req", None, None),
            P(),
            P(),
            P("req"),
        ),
        out_specs=(P("req", "head", None), P("req", "head", None)),
        check_vma=False,
    )
```

```python
import jax
import jax.numpy as jnp
from jax import lax
from jax.experimental import pallas as pl
from jax.experimental.pallas import tpu as pltpu
from jax.sharding import PartitionSpec as P

HEADS = 256
HEADDIM = 64
STATE = 256
GROUPS = 8
BLOCK = 128
AXES = ("req", "head")
MIB = 1 << 20


def partner(z=0, y=0, hi=0, lo=0, core=0):
    pairs = []
    for source in range(128):
        pairs.append((source, source ^ (lo << 6 | core << 5 | z << 3 | y << 1 | hi)))
    return pairs


def swap(array, **bits):
    return lax.ppermute(array, AXES, partner(**bits))


def flip_if(bit, array, axis):
    return jnp.where(bit == 1, jnp.flip(array, axis), array)


def conv_rows(window, previous, rows, taps):
    window[0:8, :] = previous
    window[8 : 8 + BLOCK, :] = rows
    total = window[5 : 5 + BLOCK, :] * taps[0:1, :]
    for offset in range(1, 4):
        total = total + window[5 + offset : 5 + offset + BLOCK, :] * taps[offset : offset + 1, :]
    return total * (1.0 / (1.0 + jnp.exp(-total)))


def spread(columns, lane):
    pairs = []
    for pair in range(4):
        even = columns[:, 2 * pair : 2 * pair + 1]
        odd = columns[:, 2 * pair + 1 : 2 * pair + 2]
        pairs.append(jnp.where(lane < HEADDIM, even, odd))
    return jnp.concatenate(pairs, axis=1)


def scan_kernel(
    scalars,
    x_ref,
    b_ref,
    c_ref,
    x_tail,
    b_tail,
    c_tail,
    x_taps,
    b_taps,
    c_taps,
    dt_ref,
    rate_ref,
    skip_ref,
    y_ref,
    c_out,
    decay_out,
    state_out,
    x_window,
    b_window,
    c_window,
    x_last,
    b_last,
    c_last,
    state,
    passed,
):
    request, block = pl.program_id(0), pl.program_id(1)

    @pl.when(block == 0)
    def _():
        x_last[...] = x_tail[0]
        b_last[...] = b_tail[0]
        c_last[...] = c_tail[0]
        state[...] = jnp.zeros_like(state)
        passed[...] = jnp.zeros_like(passed)

    def convolve(window, last, ref, taps):
        rows = ref[0].astype(jnp.float32)
        made = conv_rows(window, last[...], rows, taps[...].astype(jnp.float32))
        last[...] = rows[BLOCK - 8 :]
        return made.astype(jnp.bfloat16)

    x = convolve(x_window, x_last, x_ref, x_taps)
    b = convolve(b_window, b_last, b_ref, b_taps)
    c = convolve(c_window, c_last, c_ref, c_taps)
    c_out[0] = c

    place = lax.broadcasted_iota(jnp.int32, (8, BLOCK), 1)
    raw = dt_ref[0]
    step = jnp.maximum(raw, 0.0) + jnp.log1p(jnp.exp(-jnp.abs(raw)))
    step = jnp.where(place + block * BLOCK < scalars[2 + request], step, 0.0)
    decay = -rate_ref[...] * step
    reach = 1
    while reach < BLOCK:
        decay = decay + jnp.where(place >= reach, pltpu.roll(decay, reach, 1), 0.0)
        reach *= 2
    closing = decay[:, BLOCK - 1 : BLOCK]
    weight = jnp.exp(closing - decay) * step
    turned = jnp.transpose(
        jnp.concatenate(
            [decay, weight, passed[...] + decay, jnp.zeros((BLOCK - 24, BLOCK), jnp.float32)],
            axis=0,
        )
    )
    passed[...] = passed[...] + closing
    decay_out[0] = jnp.exp(turned[:, 16:24])

    lane = lax.broadcasted_iota(jnp.int32, (BLOCK, BLOCK), 1)
    causal = lax.broadcasted_iota(jnp.int32, (BLOCK, BLOCK), 0) >= lane
    scores = lax.dot_general(c, b, (((1,), (1,)), ((), ())), preferred_element_type=jnp.float32)
    scores = jnp.where(causal, scores, 0.0)
    within = []
    for pair in range(4):
        inputs = x[:, pair * 128 : (pair + 1) * 128]
        halves = []
        for head in (2 * pair, 2 * pair + 1):
            gap = jnp.where(causal, turned[:, head : head + 1] - decay[head : head + 1, :], 0.0)
            mixing = jnp.exp(gap) * scores * step[head : head + 1, :]
            halves.append(
                jnp.dot(mixing.astype(jnp.bfloat16), inputs, preferred_element_type=jnp.float32)
            )
        within.append(jnp.where(lane < HEADDIM, halves[0], halves[1]))
    carried = lax.dot_general(
        c,
        state[...].astype(jnp.bfloat16),
        (((1,), (1,)), ((), ())),
        preferred_element_type=jnp.float32,
    )
    wide = x.astype(jnp.float32)
    y_ref[0] = (
        jnp.concatenate(within, axis=1)
        + carried * spread(jnp.exp(turned[:, 0:8]), lane)
        + skip_ref[...] * wide
    )
    weighted = (wide * spread(turned[:, 8:16], lane)).astype(jnp.bfloat16)
    added = lax.dot_general(
        weighted, b, (((0,), (0,)), ((), ())), preferred_element_type=jnp.float32
    )
    factor = jnp.exp(closing)
    for head in range(8):
        rows = slice(head * HEADDIM, (head + 1) * HEADDIM)
        state[rows, :] = state[rows, :] * factor[head : head + 1, :] + added[rows, :]

    @pl.when(block == pl.num_programs(1) - 1)
    def _():
        state_out[0] = state[...]


def scan(scalars, x_input, bc_input, x_tail, bc_tail, conv_x, conv_bc, dt_raw, rate, skip):
    requests, length, width = x_input.shape
    heads = dt_raw.shape[1]

    def grouped(shape, shift):
        def at(r, i, s):
            return (r, i, s[0] + shift)

        return pl.BlockSpec(shape, at)

    def table(shift):
        return pl.BlockSpec((4, STATE), lambda r, i, s: (0, s[0] + shift))

    return pl.pallas_call(
        scan_kernel,
        grid_spec=pltpu.PrefetchScalarGridSpec(
            num_scalar_prefetch=1,
            grid=(requests, length // BLOCK),
            in_specs=[
                pl.BlockSpec((1, BLOCK, width), lambda r, i, s: (r, i, 0)),
                grouped((1, BLOCK, STATE), 0),
                grouped((1, BLOCK, STATE), GROUPS),
                pl.BlockSpec((1, 8, width), lambda r, i, s: (r, 0, 0)),
                pl.BlockSpec((1, 8, STATE), lambda r, i, s: (r, 0, 0)),
                pl.BlockSpec((1, 8, STATE), lambda r, i, s: (r, 0, 1)),
                pl.BlockSpec((4, width), lambda r, i, s: (0, 0)),
                table(0),
                table(GROUPS),
                pl.BlockSpec((1, heads, BLOCK), lambda r, i, s: (r, 0, i)),
                pl.BlockSpec((heads, 1), lambda r, i, s: (0, 0)),
                pl.BlockSpec((1, width), lambda r, i, s: (0, 0)),
            ],
            out_specs=[
                pl.BlockSpec((1, BLOCK, width), lambda r, i, s: (r, i, 0)),
                pl.BlockSpec((1, BLOCK, STATE), lambda r, i, s: (r, i, 0)),
                pl.BlockSpec((1, BLOCK, heads), lambda r, i, s: (r, i, 0)),
                pl.BlockSpec((1, width, STATE), lambda r, i, s: (r, 0, 0)),
            ],
            scratch_shapes=[
                pltpu.VMEM((8 + BLOCK, width), jnp.float32),
                pltpu.VMEM((8 + BLOCK, STATE), jnp.float32),
                pltpu.VMEM((8 + BLOCK, STATE), jnp.float32),
                pltpu.VMEM((8, width), jnp.float32),
                pltpu.VMEM((8, STATE), jnp.float32),
                pltpu.VMEM((8, STATE), jnp.float32),
                pltpu.VMEM((width, STATE), jnp.float32),
                pltpu.VMEM((heads, 1), jnp.float32),
            ],
        ),
        out_shape=[
            jax.ShapeDtypeStruct((requests, length, width), jnp.float32),
            jax.ShapeDtypeStruct((requests, length, STATE), jnp.bfloat16),
            jax.ShapeDtypeStruct((requests, length, heads), jnp.float32),
            jax.ShapeDtypeStruct((requests, width, STATE), jnp.float32),
        ],
        compiler_params=pltpu.CompilerParams(vmem_limit_bytes=32 * MIB),
        cost_estimate=pl.CostEstimate(
            flops=2 * requests * length * (8 * 128 * 128 + 2 * width * STATE + 128 * STATE),
            bytes_accessed=12 * MIB,
            transcendentals=4 * requests * length * width,
        ),
    )(
        scalars,
        x_input,
        bc_input,
        bc_input,
        x_tail,
        bc_tail,
        bc_tail,
        conv_x,
        conv_bc,
        conv_bc,
        dt_raw,
        rate,
        skip,
    )


def gate_kernel(
    scalars, y_ref, c_ref, decay_ref, part_ref, z_ref, mine, near, far, gated_ref, state_ref
):
    request = scalars[4]
    source = scalars[5]
    initial = jnp.where(source == 0, mine[...], jnp.where(source == 1, near[...], far[...]))
    lane = lax.broadcasted_iota(jnp.int32, (BLOCK, BLOCK), 1)
    narrow = initial.astype(jnp.bfloat16)
    for block in range(y_ref.shape[1] // BLOCK):
        rows = slice(block * BLOCK, (block + 1) * BLOCK)
        carried = lax.dot_general(
            c_ref[0, rows], narrow, (((1,), (1,)), ((), ())), preferred_element_type=jnp.float32
        )
        y = y_ref[0, rows] + carried * spread(decay_ref[0, rows], lane)
        z = z_ref[0, rows].astype(jnp.float32)
        position = lax.broadcasted_iota(jnp.int32, y.shape, 0) + block * BLOCK
        gated = y * (z * (1.0 / (1.0 + jnp.exp(-z))))
        gated = jnp.where(position < scalars[2 + request], gated, 0.0)
        gated = gated.astype(jnp.bfloat16).astype(jnp.float32)
        for at in range(4):
            target = (block * 4 + at) ^ scalars[1]
            gated_ref[pl.ds(pl.multiple_of(target * 32, 32), 32), :] = gated[at * 32 : at * 32 + 32]
    last = decay_ref.shape[1] - 8
    final = decay_ref[0, last:, :]
    for head in range(8):
        rows = slice(head * HEADDIM, (head + 1) * HEADDIM)
        state_ref[0, rows] = part_ref[0, rows] + initial[rows] * final[7:8, head : head + 1]


def gate(scalars, request, source, parts, z_gate, candidates):
    y, c, decay, part = parts
    _, length, width = y.shape
    scalars = jnp.concatenate([scalars, jnp.stack([jnp.int32(request), source])])

    def whole(shape):
        return pl.BlockSpec((1,) + shape, lambda i, s: (request, 0, 0))

    flat = pl.BlockSpec((width, STATE), lambda i, s: (0, 0))
    return pl.pallas_call(
        gate_kernel,
        grid_spec=pltpu.PrefetchScalarGridSpec(
            num_scalar_prefetch=1,
            grid=(1,),
            in_specs=[
                whole((length, width)),
                whole((length, STATE)),
                whole((length, decay.shape[2])),
                whole((width, STATE)),
                whole((length, width)),
                flat,
                flat,
                flat,
            ],
            out_specs=[
                pl.BlockSpec((length, width), lambda i, s: (0, 0)),
                pl.BlockSpec((1, width, STATE), lambda i, s: (0, 0, 0)),
            ],
        ),
        out_shape=[
            jax.ShapeDtypeStruct((length, width), jnp.float32),
            jax.ShapeDtypeStruct((1, width, STATE), jnp.float32),
        ],
        compiler_params=pltpu.CompilerParams(vmem_limit_bytes=32 * MIB),
        cost_estimate=pl.CostEstimate(
            flops=2 * length * width * STATE, bytes_accessed=6 * MIB, transcendentals=length * width
        ),
    )(scalars, y, c, decay, part, z_gate, *candidates)


def fetch(table, owner, slot, coords):
    _, _, _, lo, core = coords
    me = 2 * lo + core

    def entry(device, j):
        at = 2 * device + j
        return lax.dynamic_index_in_dim(table, slot[at], 0, keepdims=False), owner[at]

    away_core = 2 * lo + 1 - core
    away_chip = 2 * (1 - lo) + core
    away_both = 2 * (1 - lo) + 1 - core
    found = []
    for j in range(2):
        sent = jnp.stack([entry(away_core, j)[0], entry(away_both, j)[0]])
        got = swap(sent, core=1)
        here, holder = entry(away_chip, j)
        far = swap(jnp.where(holder == me, here, got[1]), lo=1)
        here, holder = entry(me, j)
        source = jnp.where(holder == me, 0, jnp.where(holder == away_core, 1, 2))
        found.append(((here, got[0], far), source.astype(jnp.int32)))
    return found


ORDER = ((2, 1, 0, 3), (2, 3, 0, 1))
TILE = 512
ROWS = 32


def product(blocks, w_own, w_far, y_first):
    depth, width = w_own.shape
    lines = 4 * ROWS
    side_rows = 16 * ROWS

    def kernel(own, near, cross, far, w_own_ref, w_far_ref, *rest):
        outs, own_side, far_side = rest[:6], rest[6], rest[7]

        @pl.when(pl.program_id(0) == 0)
        def _():
            own_side[:side_rows] = own[...].astype(jnp.bfloat16)
            own_side[side_rows:] = near[...].astype(jnp.bfloat16)
            far_side[:side_rows] = cross[...].astype(jnp.bfloat16)
            far_side[side_rows:] = far[...].astype(jnp.bfloat16)

        total = jnp.dot(own_side[...], w_own_ref[...], preferred_element_type=jnp.float32)
        total += jnp.dot(
            far_side[...], w_far_ref[...].astype(jnp.bfloat16), preferred_element_type=jnp.float32
        )

        def put(ref, at, major, side):
            for minor in ORDER[side]:
                z, y = (minor, major) if y_first else (major, minor)
                start = side * side_rows + (z * 4 + y) * ROWS
                ref[at * ROWS : (at + 1) * ROWS, :] = total[start : start + ROWS]
                at += 1

        put(outs[0], 0, 2, 0)
        put(outs[0], 4, 1, 0)
        put(outs[1], 0, 2, 1)
        put(outs[1], 4, 3, 1)
        put(outs[2], 0, 1, 1)
        put(outs[3], 0, 3, 0)
        put(outs[4], 0, 0, 0)
        put(outs[5], 0, 0, 1)

    heights = (2 * lines, 2 * lines, lines, lines, lines, lines)
    return pl.pallas_call(
        kernel,
        grid=(width // TILE,),
        in_specs=[pl.BlockSpec(b.shape, lambda i: (0, 0)) for b in blocks]
        + [pl.BlockSpec((depth, TILE), lambda i: (0, i))] * 2,
        out_specs=[pl.BlockSpec((h, TILE), lambda i: (0, i)) for h in heights],
        out_shape=[jax.ShapeDtypeStruct((h, width), jnp.float32) for h in heights],
        scratch_shapes=[pltpu.VMEM((2 * side_rows, depth), jnp.bfloat16)] * 2,
        compiler_params=pltpu.CompilerParams(vmem_limit_bytes=40 * MIB),
        cost_estimate=pl.CostEstimate(
            flops=2 * 4 * side_rows * depth * width,
            bytes_accessed=16 * side_rows * depth + 6 * depth * width + 8 * side_rows * width,
            transcendentals=0,
        ),
    )(*blocks, w_own, w_far)


def exchange(parts, axis):
    first, third, one_b, three_a, zero_a, zero_b = parts
    lines = one_b.shape[0]
    got1 = swap(first, **{axis: 1})
    got3 = swap(third, **{axis: 3})
    back1 = swap(one_b + got3[:lines], **{axis: 1})
    back3 = swap(three_a + got1[:lines], **{axis: 3})
    return (zero_a + got1[lines:] + back3, zero_b + got3[lines:] + back1)


def next_parts(sums):
    def rows(side, start, stop):
        chosen = [s[side][start * ROWS : stop * ROWS] for s in sums]
        if stop - start == 2:
            chosen = [c[:ROWS] for c in chosen] + [c[ROWS:] for c in chosen]
        return jnp.concatenate(chosen, axis=0)

    return (
        rows(0, 0, 2),
        rows(1, 0, 2),
        rows(1, 3, 4),
        rows(0, 3, 4),
        rows(0, 2, 3),
        rows(1, 2, 3),
    )


def far_weights(out_weight, coords):
    _, _, hi, lo, core = coords
    place = 2 * hi + lo
    width = out_weight.shape[1] // 4
    half = width // 2
    outgoing = lax.dynamic_slice_in_dim(out_weight, (3 - place) * width + core * half, half, 1)
    far_own = swap(outgoing.astype(jnp.float32), hi=1, lo=1)
    return (far_own, swap(far_own, core=1))


def project(gated, out_weight, w_far, coords):
    z, y, hi, lo, core = coords
    place = 2 * hi + lo
    width = out_weight.shape[1] // 4
    half = width // 2
    pieces = [
        lax.dynamic_slice_in_dim(out_weight, place * width + c * half, half, 1)
        for c in (core, 1 - core)
    ]
    requests = len(gated)
    first_axis = ("y", "z")
    reduced = ([], [])
    for own in gated:
        near = swap(own, lo=1)
        far = swap(own, hi=1, lo=1)
        middle = own.shape[0] // 2
        cross = jnp.concatenate(
            [swap(far[:middle], lo=1), swap(near[middle:], hi=1, lo=1)], axis=0
        )
        for c in range(2):
            parts = product((own, near, cross, far), pieces[c], w_far[c], c == 0)
            reduced[c].append(exchange(parts, first_axis[c]))
    halves = [exchange(next_parts(reduced[c]), first_axis[1 - c]) for c in range(2)]
    done = jnp.stack([jnp.stack(pair) for pair in halves]).reshape(2, 2, requests, 2, 16, half)
    kept = jnp.where(hi == 0, done[:, :, :, 0], done[:, :, :, 1])
    away = jnp.where(hi == 0, done[:, :, :, 1], done[:, :, :, 0])
    got = jnp.stack(
        [
            kept[:, 0],
            swap(kept[:, 1], lo=1),
            swap(away[:, 0], hi=1),
            swap(away[:, 1], hi=1, lo=1),
        ]
    ).reshape(2, 2, 2, requests, 16, half)
    got = flip_if(core, flip_if(lo, flip_if(hi, got, 0), 1), 2)
    return jnp.transpose(got, (3, 4, 0, 1, 2, 5)).reshape(requests, 16, 4 * width)


def on_device(
    x_input,
    z_gate,
    bc_input,
    dt_raw,
    a_log,
    d_skip,
    conv_x,
    conv_bc,
    out_weight,
    pool_state,
    pool_xtail,
    pool_bctail,
    pool_dev,
    pool_slot,
    lengths,
):
    my_req = lax.axis_index("req")
    my_head = lax.axis_index("head")
    coords = (my_head // 8, my_head // 2 % 4, my_head % 2, my_req // 2, my_req % 2)
    head_count = a_log.shape[0]
    group = my_head * head_count // (HEADS // GROUPS)
    owner = pool_dev[:, 0]

    def own_group(start):
        return lax.dynamic_slice_in_dim(pool_bctail, start * STATE, STATE, 2)

    tails = jnp.concatenate(
        [pool_xtail, own_group(group), own_group(GROUPS + group)], axis=-1
    ).astype(jnp.float32)
    tails = jnp.pad(tails, ((0, 0), (5, 0), (0, 0)))
    tail_rows = jnp.stack(
        [
            jnp.where(source == 0, mine, jnp.where(source == 1, near, far))
            for (mine, near, far), source in fetch(tails, owner, pool_slot, coords)
        ]
    )
    width = x_input.shape[2]
    w_far = far_weights(out_weight, coords)
    states = fetch(pool_state, owner, pool_slot, coords)
    scalars = jnp.concatenate([jnp.stack([group, my_head // 2]), lengths]).astype(jnp.int32)
    parts = scan(
        scalars,
        x_input,
        bc_input,
        tail_rows[:, :, :width],
        tail_rows[:, :, width:],
        conv_x,
        conv_bc,
        dt_raw,
        jnp.exp(a_log)[:, None],
        jnp.repeat(d_skip, HEADDIM)[None, :],
    )
    made = [
        gate(scalars, j, source, parts, z_gate, candidates)
        for j, (candidates, source) in enumerate(states)
    ]
    mixed_out = project([g for g, _ in made], out_weight, w_far, coords)
    return (mixed_out, jnp.concatenate([s for _, s in made], axis=0))


def solution(mesh):
    return jax.shard_map(
        on_device,
        mesh=mesh,
        in_specs=(
            P("req", None, "head"),
            P("req", None, "head"),
            P("req", None, None),
            P("req", "head", None),
            P("head"),
            P("head"),
            P(None, "head"),
            P(),
            P("head", None),
            P("req", "head", None),
            P("req", None, "head"),
            P("req", None, None),
            P(),
            P(),
            P("req"),
        ),
        out_specs=(P("req", "head", None), P("req", "head", None)),
        check_vma=False,
    )
```

```python
import functools

import jax
import jax.numpy as jnp
from jax import lax
from jax.experimental import pallas as pl
from jax.experimental.pallas import tpu as pltpu
from jax.sharding import PartitionSpec as P

HEADS = 256
HEADDIM = 64
STATE = 256
GROUPS = 8
BLOCK = 128
PARTS = 1
ROWS = 32 // PARTS
AXES = ("req", "head")
MIB = 1 << 20


def swap(array, first=0, second=0, hi=0, lo=0, core=0):
    pairs = []
    for source in range(128):
        y, z = (second, first) if source >> 5 & 1 else (first, second)
        pairs.append((source, source ^ (lo << 6 | core << 5 | z << 3 | y << 1 | hi)))
    return lax.ppermute(array, AXES, pairs)


def place_in_mesh():
    req, head = lax.axis_index("req"), lax.axis_index("head")
    return head >> 3, head >> 1 & 3, head & 1, req >> 1, req & 1


def conv_rows(window, previous, rows, taps):
    window[0:8, :] = previous
    window[8 : 8 + BLOCK, :] = rows
    total = window[5 : 5 + BLOCK, :] * taps[0:1, :]
    for offset in range(1, 4):
        total = total + window[5 + offset : 5 + offset + BLOCK, :] * taps[offset : offset + 1, :]
    return total * (1.0 / (1.0 + jnp.exp(-total)))


def spread(columns, lane):
    pairs = []
    for pair in range(4):
        even = columns[:, 2 * pair : 2 * pair + 1]
        odd = columns[:, 2 * pair + 1 : 2 * pair + 2]
        pairs.append(jnp.where(lane < HEADDIM, even, odd))
    return jnp.concatenate(pairs, axis=1)


def scan_kernel(
    lengths,
    x_ref,
    b_ref,
    c_ref,
    x_tail,
    b_tail,
    c_tail,
    x_taps,
    b_taps,
    c_taps,
    dt_ref,
    rate_ref,
    skip_ref,
    y_ref,
    c_out,
    decay_out,
    state_out,
    x_window,
    b_window,
    c_window,
    x_last,
    b_last,
    c_last,
    state,
    passed,
):
    request, block = pl.program_id(0), pl.program_id(1)

    @pl.when(block == 0)
    def _():
        x_last[...] = x_tail[0]
        b_last[...] = b_tail[0]
        c_last[...] = c_tail[0]
        state[...] = jnp.zeros_like(state)
        passed[...] = jnp.zeros_like(passed)

    def convolve(window, last, ref, taps):
        rows = ref[0].astype(jnp.float32)
        made = conv_rows(window, last[...], rows, taps[...].astype(jnp.float32))
        last[...] = rows[BLOCK - 8 :]
        return made.astype(jnp.bfloat16)

    x = convolve(x_window, x_last, x_ref, x_taps)
    b = convolve(b_window, b_last, b_ref, b_taps)
    c = convolve(c_window, c_last, c_ref, c_taps)
    c_out[0] = c

    place = lax.broadcasted_iota(jnp.int32, (8, BLOCK), 1)
    raw = dt_ref[0]
    step = jnp.maximum(raw, 0.0) + jnp.log1p(jnp.exp(-jnp.abs(raw)))
    step = jnp.where(place + block * BLOCK < lengths[request], step, 0.0)
    decay = -jnp.exp(rate_ref[...]) * step
    reach = 1
    while reach < BLOCK:
        decay = decay + jnp.where(place >= reach, pltpu.roll(decay, reach, 1), 0.0)
        reach *= 2
    closing = decay[:, BLOCK - 1 : BLOCK]
    weight = jnp.exp(closing - decay) * step
    turned = jnp.transpose(
        jnp.concatenate(
            [decay, weight, passed[...] + decay, jnp.zeros((BLOCK - 24, BLOCK), jnp.float32)],
            axis=0,
        )
    )
    passed[...] = passed[...] + closing
    decay_out[0] = jnp.exp(turned[:, 16:24])

    lane = lax.broadcasted_iota(jnp.int32, (BLOCK, BLOCK), 1)
    causal = lax.broadcasted_iota(jnp.int32, (BLOCK, BLOCK), 0) >= lane
    scores = lax.dot_general(c, b, (((1,), (1,)), ((), ())), preferred_element_type=jnp.float32)
    scores = jnp.where(causal, scores, 0.0)
    within = []
    for pair in range(4):
        inputs = x[:, pair * 128 : (pair + 1) * 128]
        halves = []
        for head in (2 * pair, 2 * pair + 1):
            gap = jnp.where(causal, turned[:, head : head + 1] - decay[head : head + 1, :], 0.0)
            mixing = jnp.exp(gap) * scores * step[head : head + 1, :]
            halves.append(
                jnp.dot(mixing.astype(jnp.bfloat16), inputs, preferred_element_type=jnp.float32)
            )
        within.append(jnp.where(lane < HEADDIM, halves[0], halves[1]))
    carried = lax.dot_general(
        c,
        state[...].astype(jnp.bfloat16),
        (((1,), (1,)), ((), ())),
        preferred_element_type=jnp.float32,
    )
    wide = x.astype(jnp.float32)
    y_ref[0] = (
        jnp.concatenate(within, axis=1)
        + carried * spread(jnp.exp(turned[:, 0:8]), lane)
        + spread(skip_ref[...], lane) * wide
    )
    weighted = (wide * spread(turned[:, 8:16], lane)).astype(jnp.bfloat16)
    added = lax.dot_general(
        weighted, b, (((0,), (0,)), ((), ())), preferred_element_type=jnp.float32
    )
    factor = jnp.exp(closing)
    for head in range(8):
        rows = slice(head * HEADDIM, (head + 1) * HEADDIM)
        state[rows, :] = state[rows, :] * factor[head : head + 1, :] + added[rows, :]

    @pl.when(block == pl.num_programs(1) - 1)
    def _():
        state_out[0] = state[...]


def scan(lengths, x_input, bc_input, tails, conv_x, conv_bc, dt_raw, a_log, d_skip):
    requests, length, width = x_input.shape
    heads = dt_raw.shape[1]

    def group():
        return lax.axis_index("head") * heads >> 5

    def grouped(shift):
        return pl.BlockSpec((1, BLOCK, STATE), lambda r, i: (r, i, group() + shift))

    def table(shift):
        return pl.BlockSpec((4, STATE), lambda r, i: (0, group() + shift))

    def tail(columns, at):
        return pl.BlockSpec((1, 8, columns), lambda r, i: (r, 0, at))

    return pl.pallas_call(
        scan_kernel,
        grid=(requests, length // BLOCK),
        in_specs=[
            pl.BlockSpec(memory_space=pltpu.SMEM),
            pl.BlockSpec((1, BLOCK, width), lambda r, i: (r, i, 0)),
            grouped(0),
            grouped(GROUPS),
            tail(width, 0),
            tail(STATE, width // STATE),
            tail(STATE, width // STATE + 1),
            pl.BlockSpec((4, width), lambda r, i: (0, 0)),
            table(0),
            table(GROUPS),
            pl.BlockSpec((1, heads, BLOCK), lambda r, i: (r, 0, i)),
            pl.BlockSpec((heads, 1), lambda r, i: (0, 0)),
            pl.BlockSpec((1, heads), lambda r, i: (0, 0)),
        ],
        out_specs=[
            pl.BlockSpec((1, BLOCK, width), lambda r, i: (r, i, 0)),
            pl.BlockSpec((1, BLOCK, STATE), lambda r, i: (r, i, 0)),
            pl.BlockSpec((1, BLOCK, heads), lambda r, i: (r, i, 0)),
            pl.BlockSpec((1, width, STATE), lambda r, i: (r, 0, 0)),
        ],
        scratch_shapes=[
            pltpu.VMEM((8 + BLOCK, width), jnp.float32),
            pltpu.VMEM((8 + BLOCK, STATE), jnp.float32),
            pltpu.VMEM((8 + BLOCK, STATE), jnp.float32),
            pltpu.VMEM((8, width), jnp.float32),
            pltpu.VMEM((8, STATE), jnp.float32),
            pltpu.VMEM((8, STATE), jnp.float32),
            pltpu.VMEM((width, STATE), jnp.float32),
            pltpu.VMEM((heads, 1), jnp.float32),
        ],
        out_shape=[
            jax.ShapeDtypeStruct((requests, length, width), jnp.float32),
            jax.ShapeDtypeStruct((requests, length, STATE), jnp.bfloat16),
            jax.ShapeDtypeStruct((requests, length, heads), jnp.float32),
            jax.ShapeDtypeStruct((requests, width, STATE), jnp.float32),
        ],
        compiler_params=pltpu.CompilerParams(vmem_limit_bytes=56 * MIB),
        cost_estimate=pl.CostEstimate(
            flops=2 * requests * length * (8 * 128 * 128 + 2 * width * STATE + 128 * STATE),
            bytes_accessed=12 * MIB,
            transcendentals=4 * requests * length * width,
        ),
    )(
        lengths,
        x_input,
        bc_input,
        bc_input,
        tails,
        tails,
        tails,
        conv_x,
        conv_bc,
        conv_bc,
        dt_raw,
        a_log[:, None],
        d_skip[None, :],
    )


def prepare_kernel(
    owner, slot, pool, tails, weight, away_0, away_1, mine, chip, tail_away, tail_mine, tail_chip,
    outgoing, columns, semaphore
):
    _, _, hi, lo, core = place_in_mesh()
    half = columns.shape[1]
    start = ((3 - 2 * hi - lo) * 2 + core) * half
    copy = pltpu.make_async_copy(
        weight.at[:, pl.ds(pl.multiple_of(start, half), half)], columns, semaphore
    )
    copy.start()
    me = 2 * lo + core
    for j in range(2):
        away = (away_0, away_1)[j]
        for device, state, tail in (
            (me ^ 1, away.at[0], tail_away.at[j, 0]),
            (me ^ 3, away.at[1], tail_away.at[j, 1]),
            (me ^ 2, chip.at[j], tail_chip.at[j]),
            (me, mine.at[j], tail_mine.at[j]),
        ):
            request = 2 * device + j
            here = owner[request, 0] == me
            at = slot[request]
            state[...] = jnp.where(here, pool[at], 0.0)
            tail[...] = jnp.where(here, tails[at], 0.0)
    copy.wait()
    outgoing[...] = columns[...].astype(jnp.float32)


def prepare(owner, slot, pool, tails, weight):
    _, width, state = pool.shape
    columns = tails.shape[2]
    half = weight.shape[1] // 8
    vmem = pl.BlockSpec(memory_space=pltpu.VMEM)
    smem = pl.BlockSpec(memory_space=pltpu.SMEM)
    shapes = (
        (2, width, state),
        (2, width, state),
        (2, width, state),
        (2, width, state),
        (2, 2, 8, columns),
        (2, 8, columns),
        (2, 8, columns),
        (weight.shape[0], half),
    )
    return pl.pallas_call(
        prepare_kernel,
        in_specs=[smem, smem, vmem, vmem, pl.BlockSpec(memory_space=pl.ANY)],
        out_specs=[vmem] * len(shapes),
        out_shape=[jax.ShapeDtypeStruct(s, jnp.float32) for s in shapes],
        scratch_shapes=[
            pltpu.VMEM((weight.shape[0], half), weight.dtype),
            pltpu.SemaphoreType.DMA,
        ],
        compiler_params=pltpu.CompilerParams(vmem_limit_bytes=48 * MIB),
        cost_estimate=pl.CostEstimate(flops=0, bytes_accessed=10 * MIB, transcendentals=0),
    )(owner, slot, pool, tails, weight)


def gate_kernel(
    lengths, y_ref, c_ref, decay_ref, part_ref, z_ref, mine, near, far, *outs, request
):
    z_at, y_at, _, _, core = place_in_mesh()
    gated_refs, state_ref = outs[:PARTS], outs[PARTS]
    initial = mine[0] + near[0] + far[...]
    lane = lax.broadcasted_iota(jnp.int32, (BLOCK, BLOCK), 1)
    narrow = initial.astype(jnp.bfloat16)
    for block in range(y_ref.shape[1] // BLOCK):
        rows = slice(block * BLOCK, (block + 1) * BLOCK)
        carried = lax.dot_general(
            c_ref[0, rows], narrow, (((1,), (1,)), ((), ())), preferred_element_type=jnp.float32
        )
        y = y_ref[0, rows] + carried * spread(decay_ref[0, rows], lane)
        z = z_ref[0, rows].astype(jnp.float32)
        position = lax.broadcasted_iota(jnp.int32, y.shape, 0) + block * BLOCK
        gated = y * (z * (1.0 / (1.0 + jnp.exp(-z))))
        gated = jnp.where(position < lengths[request], gated, 0.0)
        gated = gated.astype(jnp.bfloat16).astype(jnp.float32)
        for at in range(4):
            z_far, y_far = block ^ z_at, at ^ y_at
            target = jnp.where(core == 0, y_far * 4 + z_far, z_far * 4 + y_far) * ROWS
            for part in range(PARTS):
                start = at * 32 + part * ROWS
                gated_refs[part][pl.ds(pl.multiple_of(target, ROWS), ROWS), :] = gated[
                    start : start + ROWS
                ]
    last = decay_ref.shape[1] - 8
    final = decay_ref[0, last:, :]
    for head in range(8):
        rows = slice(head * HEADDIM, (head + 1) * HEADDIM)
        state_ref[0, rows] = part_ref[0, rows] + initial[rows] * final[7:8, head : head + 1]


def gate(lengths, request, parts, z_gate, mine, near, far):
    y, c, decay, part = parts
    _, length, width = y.shape

    def whole(shape, at):
        return pl.BlockSpec((1,) + shape, lambda i: (at, 0, 0))

    return pl.pallas_call(
        functools.partial(gate_kernel, request=request),
        grid=(1,),
        in_specs=[
            pl.BlockSpec(memory_space=pltpu.SMEM),
            whole((length, width), request),
            whole((length, STATE), request),
            whole((length, decay.shape[2]), request),
            whole((width, STATE), request),
            whole((length, width), request),
            whole((width, STATE), request),
            whole((width, STATE), 0),
            pl.BlockSpec((width, STATE), lambda i: (0, 0)),
        ],
        out_specs=[pl.BlockSpec((length // PARTS, width), lambda i: (0, 0))] * PARTS
        + [whole((width, STATE), 0)],
        out_shape=[jax.ShapeDtypeStruct((length // PARTS, width), jnp.float32)] * PARTS
        + [jax.ShapeDtypeStruct((1, width, STATE), jnp.float32)],
        compiler_params=pltpu.CompilerParams(vmem_limit_bytes=48 * MIB),
        cost_estimate=pl.CostEstimate(
            flops=2 * length * width * STATE, bytes_accessed=6 * MIB, transcendentals=length * width
        ),
    )(lengths, y, c, decay, part, z_gate, mine, near, far)


ORDER = ((2, 1, 0, 3), (2, 3, 0, 1))
TILE = 512


def product(blocks, weight, w_far):
    depth, half = w_far[0].shape
    lines = 4 * ROWS
    side_rows = 16 * ROWS
    tiles = half // TILE

    def kernel(own, near, cross_near, cross_far, far, w_own_ref, w_near_ref, w_far_ref, *rest):
        outs, own_side, far_side, far_weight = rest[:6], rest[6], rest[7], rest[8]
        step = pl.program_id(0)

        @pl.when(step == 0)
        def _():
            middle = side_rows // 2
            own_side[:side_rows] = own[...].astype(jnp.bfloat16)
            own_side[side_rows:] = near[...].astype(jnp.bfloat16)
            far_side[:middle] = cross_near[...].astype(jnp.bfloat16)
            far_side[middle:side_rows] = cross_far[...].astype(jnp.bfloat16)
            far_side[side_rows:] = far[...].astype(jnp.bfloat16)

        @pl.when(step < tiles)
        def _():
            far_weight[...] = w_near_ref[...].astype(jnp.bfloat16)

        @pl.when(step >= tiles)
        def _():
            far_weight[...] = w_far_ref[...].astype(jnp.bfloat16)

        total = jnp.dot(own_side[...], w_own_ref[...], preferred_element_type=jnp.float32)
        total += jnp.dot(far_side[...], far_weight[...], preferred_element_type=jnp.float32)

        def put(ref, at, major, side):
            for minor in ORDER[side]:
                start = side * side_rows + (major * 4 + minor) * ROWS
                ref[at * ROWS : (at + 1) * ROWS, :] = total[start : start + ROWS]
                at += 1

        put(outs[0], 0, 2, 0)
        put(outs[0], 4, 1, 0)
        put(outs[1], 0, 2, 1)
        put(outs[1], 4, 3, 1)
        put(outs[2], 0, 1, 1)
        put(outs[3], 0, 3, 0)
        put(outs[4], 0, 0, 0)
        put(outs[5], 0, 0, 1)

    def own_columns(i):
        _, _, hi, lo, core = place_in_mesh()
        side = jnp.where(i < tiles, core, 1 - core)
        return (0, ((2 * hi + lo) * 2 + side) * tiles + jnp.where(i < tiles, i, i - tiles))

    heights = (2 * lines, 2 * lines, lines, lines, lines, lines)
    return pl.pallas_call(
        kernel,
        grid=(2 * tiles,),
        in_specs=[pl.BlockSpec(b.shape, lambda i: (0, 0)) for b in blocks]
        + [
            pl.BlockSpec((depth, TILE), own_columns),
            pl.BlockSpec((depth, TILE), lambda i: (0, jnp.minimum(i, tiles - 1))),
            pl.BlockSpec((depth, TILE), lambda i: (0, jnp.maximum(i - tiles, 0))),
        ],
        out_specs=[pl.BlockSpec((h, TILE), lambda i: (0, i)) for h in heights],
        out_shape=[jax.ShapeDtypeStruct((h, 2 * half), jnp.float32) for h in heights],
        scratch_shapes=[pltpu.VMEM((2 * side_rows, depth), jnp.bfloat16)] * 2
        + [pltpu.VMEM((depth, TILE), jnp.bfloat16)],
        compiler_params=pltpu.CompilerParams(vmem_limit_bytes=48 * MIB),
        cost_estimate=pl.CostEstimate(
            flops=8 * side_rows * depth * 2 * half,
            bytes_accessed=16 * side_rows * depth + 12 * depth * half + 16 * side_rows * half,
            transcendentals=0,
        ),
    )(*blocks, weight, *w_far)


def exchange(parts, axis):
    first, third, one_b, three_a, zero_a, zero_b = parts
    lines = one_b.shape[0]
    got1 = swap(first, **{axis: 1})
    got3 = swap(third, **{axis: 3})
    back1 = swap(one_b + got3[:lines], **{axis: 1})
    back3 = swap(three_a + got1[:lines], **{axis: 3})
    return ((zero_a, got1, back3), (zero_b, got3, back1))


def next_parts(chunks):
    def rows(side, start, stop):
        chosen = []
        for chunk in chunks:
            kept, got, back = chunk[side]
            lines = kept.shape[0]
            span = slice(start * ROWS, stop * ROWS)
            after = slice(lines + start * ROWS, lines + stop * ROWS)
            chosen.append(kept[span] + got[after] + back[span])
        if stop - start == 2:
            chosen = [c[:ROWS] for c in chosen] + [c[ROWS:] for c in chosen]
        return jnp.concatenate(chosen, axis=0)

    return (
        rows(0, 0, 2),
        rows(1, 0, 2),
        rows(1, 3, 4),
        rows(0, 3, 4),
        rows(0, 2, 3),
        rows(1, 2, 3),
    )


def finish_kernel(kept_0, got_0, back_0, kept_1, got_1, back_1, *outs):
    hi = lax.axis_index("head") & 1
    for side, (kept, got, back) in enumerate(((kept_0, got_0, back_0), (kept_1, got_1, back_1))):
        lines = kept.shape[0]
        for request in range(2):
            for way in range(2):
                part = hi ^ way
                row = pl.multiple_of(request * 32 + part * 16, 16)
                later = pl.multiple_of(lines + request * 32 + part * 16, 16)
                outs[2 * way + side][request] = (
                    kept[pl.ds(row, 16), :] + got[pl.ds(later, 16), :] + back[pl.ds(row, 16), :]
                )


def finish(sides):
    columns = sides[0][0].shape[1]
    vmem = pl.BlockSpec(memory_space=pltpu.VMEM)
    return pl.pallas_call(
        finish_kernel,
        in_specs=[vmem] * 6,
        out_specs=[vmem] * 4,
        out_shape=[jax.ShapeDtypeStruct((2, 16, columns), jnp.float32)] * 4,
        compiler_params=pltpu.CompilerParams(vmem_limit_bytes=32 * MIB),
        cost_estimate=pl.CostEstimate(flops=0, bytes_accessed=4 * MIB, transcendentals=0),
    )(*sides[0], *sides[1])


def assemble_kernel(own, near, across, far, mixed):
    _, _, hi, lo, core = place_in_mesh()
    half = own.shape[2] // 2
    for flip, source in enumerate((own, near, across, far)):
        place = (2 * hi + lo) ^ flip
        for side in range(2):
            start = pl.multiple_of((place * 2 + (side ^ core)) * half, half)
            mixed[:, :, pl.ds(start, half)] = source[:, :, side * half : (side + 1) * half]


def assemble(pieces):
    requests, rows, columns = pieces[0].shape
    vmem = pl.BlockSpec(memory_space=pltpu.VMEM)
    return pl.pallas_call(
        assemble_kernel,
        in_specs=[vmem] * 4,
        out_specs=vmem,
        out_shape=jax.ShapeDtypeStruct((requests, rows, 4 * columns), jnp.float32),
        compiler_params=pltpu.CompilerParams(vmem_limit_bytes=32 * MIB),
        cost_estimate=pl.CostEstimate(flops=0, bytes_accessed=2 * MIB, transcendentals=0),
    )(*pieces)


def project(gated, out_weight, w_far):
    chunks = []
    for own in gated:
        near = swap(own, lo=1)
        far = swap(own, hi=1, lo=1)
        middle = own.shape[0] // 2
        cross_near = swap(far[:middle], lo=1)
        cross_far = swap(near[middle:], hi=1, lo=1)
        parts = product((own, near, cross_near, cross_far, far), out_weight, w_far)
        chunks.append(exchange(parts, "first"))
    kept_0, kept_1, away_0, away_1 = finish(exchange(next_parts(chunks), "second"))
    return assemble(
        (kept_0, swap(kept_1, lo=1), swap(away_0, hi=1), swap(away_1, hi=1, lo=1))
    )


def on_device(
    x_input,
    z_gate,
    bc_input,
    dt_raw,
    a_log,
    d_skip,
    conv_x,
    conv_bc,
    out_weight,
    pool_state,
    pool_xtail,
    pool_bctail,
    pool_dev,
    pool_slot,
    lengths,
):
    group = lax.axis_index("head").astype(jnp.uint32) * a_log.shape[0] >> 5
    bc_tail = pool_bctail.reshape(pool_bctail.shape[:2] + (2, GROUPS, STATE))
    bc_tail = lax.dynamic_index_in_dim(bc_tail, group, 3, keepdims=False)
    tails = jnp.concatenate([pool_xtail, bc_tail.reshape(bc_tail.shape[:2] + (2 * STATE,))], axis=-1)
    tails = jnp.pad(tails.astype(jnp.float32), ((0, 0), (5, 0), (0, 0)))
    away_0, away_1, mine, chip, tail_away, tail_mine, tail_chip, outgoing = prepare(
        pool_dev, pool_slot, pool_state, tails, out_weight
    )
    tail_near = swap(tail_away, core=1)
    tail_far = swap(tail_chip + tail_near[:, 1], lo=1)
    tail_rows = tail_mine + tail_near[:, 0] + tail_far
    w_near = swap(outgoing, hi=1, lo=1)
    w_far = (w_near, swap(w_near, core=1))
    parts = scan(
        lengths, x_input, bc_input, tail_rows, conv_x, conv_bc, dt_raw, a_log, d_skip
    )
    gated, closing = [], []
    for j, away in enumerate((away_0, away_1)):
        near = swap(away, core=1)
        far = swap(chip[j] + near[1], lo=1)
        *rows, state = gate(lengths, j, parts, z_gate, mine, near, far)
        gated += rows
        closing.append(state)
    mixed_out = project(gated, out_weight, w_far)
    return (mixed_out, jnp.concatenate(closing, axis=0))


def solution(mesh):
    return jax.shard_map(
        on_device,
        mesh=mesh,
        in_specs=(
            P("req", None, "head"),
            P("req", None, "head"),
            P("req", None, None),
            P("req", "head", None),
            P("head"),
            P("head"),
            P(None, "head"),
            P(),
            P("head", None),
            P("req", "head", None),
            P("req", None, "head"),
            P("req", None, None),
            P(),
            P(),
            P("req"),
        ),
        out_specs=(P("req", "head", None), P("req", "head", None)),
        check_vma=False,
    )
```

```python
import functools

import jax
import jax.numpy as jnp
from jax import lax
from jax.experimental import pallas as pl
from jax.experimental.pallas import tpu as pltpu
from jax.sharding import PartitionSpec as P

HEADS = 256
HEADDIM = 64
STATE = 256
GROUPS = 8
BLOCK = 128
PARTS = 2
ROWS = 32 // PARTS
AXES = ("req", "head")
MIB = 1 << 20


def swap(array, first=0, second=0, hi=0, lo=0, core=0):
    pairs = []
    for source in range(128):
        y, z = (second, first) if source >> 5 & 1 else (first, second)
        pairs.append((source, source ^ (lo << 6 | core << 5 | z << 3 | y << 1 | hi)))
    return lax.ppermute(array, AXES, pairs)


def after(array, *others):
    return lax.optimization_barrier((array,) + others)[0]


def cross(near, far):
    pairs = []
    for source in range(128):
        pairs.append((source, source ^ (64 | (source >> 5 & 1))))
    core = lax.axis_index("req") & 1
    return lax.ppermute(jnp.where(core == 0, far, near), AXES, pairs)


def place_in_mesh():
    req, head = lax.axis_index("req"), lax.axis_index("head")
    return head >> 3, head >> 1 & 3, head & 1, req >> 1, req & 1


def conv_rows(window, previous, rows, taps):
    window[0:8, :] = previous
    window[8 : 8 + BLOCK, :] = rows
    total = window[5 : 5 + BLOCK, :] * taps[0:1, :]
    for offset in range(1, 4):
        total = total + window[5 + offset : 5 + offset + BLOCK, :] * taps[offset : offset + 1, :]
    return total * (1.0 / (1.0 + jnp.exp(-total)))


def spread(columns, lane):
    pairs = []
    for pair in range(4):
        even = columns[:, 2 * pair : 2 * pair + 1]
        odd = columns[:, 2 * pair + 1 : 2 * pair + 2]
        pairs.append(jnp.where(lane < HEADDIM, even, odd))
    return jnp.concatenate(pairs, axis=1)


def scan_kernel(
    lengths,
    x_ref,
    b_ref,
    c_ref,
    x_tail,
    b_tail,
    c_tail,
    x_taps,
    b_taps,
    c_taps,
    dt_ref,
    rate_ref,
    skip_ref,
    y_ref,
    c_out,
    decay_out,
    state_out,
    x_window,
    b_window,
    c_window,
    x_last,
    b_last,
    c_last,
    state,
    passed,
):
    request, block = pl.program_id(0), pl.program_id(1)

    @pl.when(block == 0)
    def _():
        x_last[...] = x_tail[0]
        b_last[...] = b_tail[0]
        c_last[...] = c_tail[0]
        state[...] = jnp.zeros_like(state)
        passed[...] = jnp.zeros_like(passed)

    def convolve(window, last, ref, taps):
        rows = ref[0].astype(jnp.float32)
        made = conv_rows(window, last[...], rows, taps[...].astype(jnp.float32))
        last[...] = rows[BLOCK - 8 :]
        return made.astype(jnp.bfloat16)

    x = convolve(x_window, x_last, x_ref, x_taps)
    b = convolve(b_window, b_last, b_ref, b_taps)
    c = convolve(c_window, c_last, c_ref, c_taps)
    c_out[0] = c

    place = lax.broadcasted_iota(jnp.int32, (8, BLOCK), 1)
    raw = dt_ref[0]
    step = jnp.maximum(raw, 0.0) + jnp.log1p(jnp.exp(-jnp.abs(raw)))
    step = jnp.where(place + block * BLOCK < lengths[request], step, 0.0)
    decay = -jnp.exp(rate_ref[...]) * step
    reach = 1
    while reach < BLOCK:
        decay = decay + jnp.where(place >= reach, pltpu.roll(decay, reach, 1), 0.0)
        reach *= 2
    closing = decay[:, BLOCK - 1 : BLOCK]
    weight = jnp.exp(closing - decay) * step
    turned = jnp.transpose(
        jnp.concatenate(
            [decay, weight, passed[...] + decay, jnp.zeros((BLOCK - 24, BLOCK), jnp.float32)],
            axis=0,
        )
    )
    passed[...] = passed[...] + closing
    decay_out[0] = jnp.exp(turned[:, 16:24])

    lane = lax.broadcasted_iota(jnp.int32, (BLOCK, BLOCK), 1)
    causal = lax.broadcasted_iota(jnp.int32, (BLOCK, BLOCK), 0) >= lane
    scores = lax.dot_general(c, b, (((1,), (1,)), ((), ())), preferred_element_type=jnp.float32)
    scores = jnp.where(causal, scores, 0.0)
    within = []
    for pair in range(4):
        inputs = x[:, pair * 128 : (pair + 1) * 128]
        halves = []
        for head in (2 * pair, 2 * pair + 1):
            gap = jnp.where(causal, turned[:, head : head + 1] - decay[head : head + 1, :], 0.0)
            mixing = jnp.exp(gap) * scores * step[head : head + 1, :]
            halves.append(
                jnp.dot(mixing.astype(jnp.bfloat16), inputs, preferred_element_type=jnp.float32)
            )
        within.append(jnp.where(lane < HEADDIM, halves[0], halves[1]))
    carried = lax.dot_general(
        c,
        state[...].astype(jnp.bfloat16),
        (((1,), (1,)), ((), ())),
        preferred_element_type=jnp.float32,
    )
    wide = x.astype(jnp.float32)
    y_ref[0] = (
        jnp.concatenate(within, axis=1)
        + carried * spread(jnp.exp(turned[:, 0:8]), lane)
        + spread(skip_ref[...], lane) * wide
    )
    weighted = (wide * spread(turned[:, 8:16], lane)).astype(jnp.bfloat16)
    added = lax.dot_general(
        weighted, b, (((0,), (0,)), ((), ())), preferred_element_type=jnp.float32
    )
    factor = jnp.exp(closing)
    for head in range(8):
        rows = slice(head * HEADDIM, (head + 1) * HEADDIM)
        state[rows, :] = state[rows, :] * factor[head : head + 1, :] + added[rows, :]

    @pl.when(block == pl.num_programs(1) - 1)
    def _():
        state_out[0] = state[...]


def scan(lengths, x_input, bc_input, tails, conv_x, conv_bc, dt_raw, a_log, d_skip):
    requests, length, width = x_input.shape
    heads = dt_raw.shape[1]

    def group():
        return lax.axis_index("head") * heads >> 5

    def grouped(shift):
        return pl.BlockSpec((1, BLOCK, STATE), lambda r, i: (r, i, group() + shift))

    def table(shift):
        return pl.BlockSpec((4, STATE), lambda r, i: (0, group() + shift))

    def tail(columns, at):
        return pl.BlockSpec((1, 8, columns), lambda r, i: (r, 0, at))

    return pl.pallas_call(
        scan_kernel,
        grid=(requests, length // BLOCK),
        in_specs=[
            pl.BlockSpec(memory_space=pltpu.SMEM),
            pl.BlockSpec((1, BLOCK, width), lambda r, i: (r, i, 0)),
            grouped(0),
            grouped(GROUPS),
            tail(width, 0),
            tail(STATE, width // STATE),
            tail(STATE, width // STATE + 1),
            pl.BlockSpec((4, width), lambda r, i: (0, 0)),
            table(0),
            table(GROUPS),
            pl.BlockSpec((1, heads, BLOCK), lambda r, i: (r, 0, i)),
            pl.BlockSpec((heads, 1), lambda r, i: (0, 0)),
            pl.BlockSpec((1, heads), lambda r, i: (0, 0)),
        ],
        out_specs=[
            pl.BlockSpec((1, BLOCK, width), lambda r, i: (r, i, 0)),
            pl.BlockSpec((1, BLOCK, STATE), lambda r, i: (r, i, 0)),
            pl.BlockSpec((1, BLOCK, heads), lambda r, i: (r, i, 0)),
            pl.BlockSpec((1, width, STATE), lambda r, i: (r, 0, 0)),
        ],
        scratch_shapes=[
            pltpu.VMEM((8 + BLOCK, width), jnp.float32),
            pltpu.VMEM((8 + BLOCK, STATE), jnp.float32),
            pltpu.VMEM((8 + BLOCK, STATE), jnp.float32),
            pltpu.VMEM((8, width), jnp.float32),
            pltpu.VMEM((8, STATE), jnp.float32),
            pltpu.VMEM((8, STATE), jnp.float32),
            pltpu.VMEM((width, STATE), jnp.float32),
            pltpu.VMEM((heads, 1), jnp.float32),
        ],
        out_shape=[
            jax.ShapeDtypeStruct((requests, length, width), jnp.float32),
            jax.ShapeDtypeStruct((requests, length, STATE), jnp.bfloat16),
            jax.ShapeDtypeStruct((requests, length, heads), jnp.float32),
            jax.ShapeDtypeStruct((requests, width, STATE), jnp.float32),
        ],
        compiler_params=pltpu.CompilerParams(vmem_limit_bytes=56 * MIB),
        cost_estimate=pl.CostEstimate(
            flops=2 * requests * length * (8 * 128 * 128 + 2 * width * STATE + 128 * STATE),
            bytes_accessed=12 * MIB,
            transcendentals=4 * requests * length * width,
        ),
    )(
        lengths,
        x_input,
        bc_input,
        bc_input,
        tails,
        tails,
        tails,
        conv_x,
        conv_bc,
        conv_bc,
        dt_raw,
        a_log[:, None],
        d_skip[None, :],
    )


def outgoing_kernel(weight, outgoing, columns, semaphore):
    _, _, hi, lo, core = place_in_mesh()
    half = columns.shape[1]
    start = pl.multiple_of(((3 - 2 * hi - lo) * 2 + core) * half, half)
    copy = pltpu.make_async_copy(weight.at[:, pl.ds(start, half)], columns, semaphore)
    copy.start()
    copy.wait()
    outgoing[...] = columns[...].astype(jnp.float32)


def outgoing_weights(weight):
    half = weight.shape[1] // 8
    return pl.pallas_call(
        outgoing_kernel,
        in_specs=[pl.BlockSpec(memory_space=pl.ANY)],
        out_specs=pl.BlockSpec(memory_space=pltpu.VMEM),
        out_shape=jax.ShapeDtypeStruct((weight.shape[0], half), jnp.float32),
        scratch_shapes=[
            pltpu.VMEM((weight.shape[0], half), weight.dtype),
            pltpu.SemaphoreType.DMA,
        ],
        compiler_params=pltpu.CompilerParams(vmem_limit_bytes=48 * MIB),
        cost_estimate=pl.CostEstimate(flops=0, bytes_accessed=3 * MIB, transcendentals=0),
    )(weight)


def prepare_kernel(
    owner, slot, pool, tails, away_0, away_1, mine, chip, tail_away, tail_mine, tail_chip
):
    _, _, _, lo, core = place_in_mesh()
    me = 2 * lo + core
    for j in range(2):
        away = (away_0, away_1)[j]
        for device, state, tail in (
            (me ^ 1, away.at[0], tail_away.at[j, 0]),
            (me ^ 3, away.at[1], tail_away.at[j, 1]),
            (me ^ 2, chip.at[j], tail_chip.at[j]),
            (me, mine.at[j], tail_mine.at[j]),
        ):
            request = 2 * device + j
            here = owner[request] == me
            at = slot[request]
            state[...] = jnp.where(here, pool[at], 0.0)
            tail[...] = jnp.where(here, tails[at], 0.0)


def prepare(owner, slot, pool, tails):
    _, width, state = pool.shape
    columns = tails.shape[2]
    vmem = pl.BlockSpec(memory_space=pltpu.VMEM)
    smem = pl.BlockSpec(memory_space=pltpu.SMEM)
    shapes = (
        (2, width, state),
        (2, width, state),
        (2, width, state),
        (2, width, state),
        (2, 2, 8, columns),
        (2, 8, columns),
        (2, 8, columns),
    )
    return pl.pallas_call(
        prepare_kernel,
        in_specs=[smem, smem, vmem, vmem],
        out_specs=[vmem] * len(shapes),
        out_shape=[jax.ShapeDtypeStruct(s, jnp.float32) for s in shapes],
        compiler_params=pltpu.CompilerParams(vmem_limit_bytes=48 * MIB),
        cost_estimate=pl.CostEstimate(flops=0, bytes_accessed=7 * MIB, transcendentals=0),
    )(owner, slot, pool, tails)


def gate_kernel(
    lengths, y_ref, c_ref, decay_ref, part_ref, z_ref, mine, near, far, *outs, request
):
    z_at, y_at, _, _, core = place_in_mesh()
    gated_refs, state_ref = outs[:PARTS], outs[PARTS]
    initial = mine[0] + near[0] + far[...]
    lane = lax.broadcasted_iota(jnp.int32, (BLOCK, BLOCK), 1)
    narrow = initial.astype(jnp.bfloat16)
    for block in range(y_ref.shape[1] // BLOCK):
        rows = slice(block * BLOCK, (block + 1) * BLOCK)
        carried = lax.dot_general(
            c_ref[0, rows], narrow, (((1,), (1,)), ((), ())), preferred_element_type=jnp.float32
        )
        y = y_ref[0, rows] + carried * spread(decay_ref[0, rows], lane)
        z = z_ref[0, rows].astype(jnp.float32)
        position = lax.broadcasted_iota(jnp.int32, y.shape, 0) + block * BLOCK
        gated = y * (z * (1.0 / (1.0 + jnp.exp(-z))))
        gated = jnp.where(position < lengths[request], gated, 0.0)
        gated = gated.astype(jnp.bfloat16).astype(jnp.float32)
        for at in range(4):
            z_far, y_far = block ^ z_at, at ^ y_at
            target = jnp.where(core == 0, y_far * 4 + z_far, z_far * 4 + y_far) * ROWS
            for part in range(PARTS):
                start = at * 32 + part * ROWS
                gated_refs[part][pl.ds(pl.multiple_of(target, ROWS), ROWS), :] = gated[
                    start : start + ROWS
                ]
    last = decay_ref.shape[1] - 8
    final = decay_ref[0, last:, :]
    for head in range(8):
        rows = slice(head * HEADDIM, (head + 1) * HEADDIM)
        state_ref[0, rows] = part_ref[0, rows] + initial[rows] * final[7:8, head : head + 1]


def gate(lengths, request, parts, z_gate, mine, near, far):
    y, c, decay, part = parts
    _, length, width = y.shape

    def whole(shape, at):
        return pl.BlockSpec((1,) + shape, lambda i: (at, 0, 0))

    return pl.pallas_call(
        functools.partial(gate_kernel, request=request),
        grid=(1,),
        in_specs=[
            pl.BlockSpec(memory_space=pltpu.SMEM),
            whole((length, width), request),
            whole((length, STATE), request),
            whole((length, decay.shape[2]), request),
            whole((width, STATE), request),
            whole((length, width), request),
            whole((width, STATE), request),
            whole((width, STATE), 0),
            pl.BlockSpec((width, STATE), lambda i: (0, 0)),
        ],
        out_specs=[pl.BlockSpec((length // PARTS, width), lambda i: (0, 0))] * PARTS
        + [whole((width, STATE), 0)],
        out_shape=[jax.ShapeDtypeStruct((length // PARTS, width), jnp.float32)] * PARTS
        + [jax.ShapeDtypeStruct((1, width, STATE), jnp.float32)],
        compiler_params=pltpu.CompilerParams(vmem_limit_bytes=48 * MIB),
        cost_estimate=pl.CostEstimate(
            flops=2 * length * width * STATE, bytes_accessed=6 * MIB, transcendentals=length * width
        ),
    )(lengths, y, c, decay, part, z_gate, mine, near, far)


ORDER = ((2, 1, 0, 3), (2, 3, 0, 1))
TILE = 512


def product(blocks, weight, w_far, before):
    depth = weight.shape[0]
    width = weight.shape[1] // 4
    lines = 4 * ROWS
    side_rows = 16 * ROWS
    tiles = width // (2 * TILE)
    opening = not before

    def kernel(*refs):
        own, near, opposite, far, w_own_ref = refs[:5]
        inputs, outs = refs[5 : -2 - 6 - opening], refs[-2 - 6 - opening : -2]
        own_side, far_side = refs[-2:]
        step = pl.program_id(0)

        @pl.when(step == 0)
        def _():
            own_side[:side_rows] = own[...].astype(jnp.bfloat16)
            own_side[side_rows:] = near[...].astype(jnp.bfloat16)
            far_side[:side_rows] = opposite[...].astype(jnp.bfloat16)
            far_side[side_rows:] = far[...].astype(jnp.bfloat16)

        if opening:
            far_weight = outs[6]

            @pl.when(step < tiles)
            def _():
                far_weight[...] = inputs[0][...].astype(jnp.bfloat16)

            @pl.when(step >= tiles)
            def _():
                far_weight[...] = inputs[1][...].astype(jnp.bfloat16)
        else:
            far_weight, got1, got3, one_b, three_a = inputs
            outs[0][2 * lines :, :] = one_b[...] + got3[...]
            outs[1][2 * lines :, :] = three_a[...] + got1[...]

        total = jnp.dot(own_side[...], w_own_ref[...], preferred_element_type=jnp.float32)
        total += jnp.dot(far_side[...], far_weight[...], preferred_element_type=jnp.float32)

        def put(ref, at, major, side):
            for minor in ORDER[side]:
                start = side * side_rows + (major * 4 + minor) * ROWS
                ref[at * ROWS : (at + 1) * ROWS, :] = total[start : start + ROWS]
                at += 1

        put(outs[0], 0, 2, 0)
        put(outs[0], 4, 1, 0)
        put(outs[1], 0, 2, 1)
        put(outs[1], 4, 3, 1)
        put(outs[2], 0, 1, 1)
        put(outs[3], 0, 3, 0)
        put(outs[4], 0, 0, 0)
        put(outs[5], 0, 0, 1)

    def own_columns(i):
        _, _, hi, lo, core = place_in_mesh()
        side = jnp.where(i < tiles, core, 1 - core)
        return (0, ((2 * hi + lo) * 2 + side) * tiles + jnp.where(i < tiles, i, i - tiles))

    def tile(rows):
        return pl.BlockSpec((rows, TILE), lambda i: (0, i))

    if opening:
        extra_specs = [
            pl.BlockSpec((depth, TILE), lambda i: (0, jnp.minimum(i, tiles - 1))),
            pl.BlockSpec((depth, TILE), lambda i: (0, jnp.maximum(i - tiles, 0))),
        ]
        extra = w_far
    else:
        extra_specs = [tile(depth)] + [tile(lines)] * 4
        extra = (w_far,) + before
    sent = 2 * lines if opening else 3 * lines
    heights = (sent, sent, lines, lines, lines, lines)
    out_specs = [tile(h) for h in heights]
    out_shape = [jax.ShapeDtypeStruct((h, width), jnp.float32) for h in heights]
    if opening:
        out_specs.append(tile(depth))
        out_shape.append(jax.ShapeDtypeStruct((depth, width), jnp.bfloat16))
    return pl.pallas_call(
        kernel,
        grid=(2 * tiles,),
        in_specs=[pl.BlockSpec(b.shape, lambda i: (0, 0)) for b in blocks]
        + [pl.BlockSpec((depth, TILE), own_columns)]
        + extra_specs,
        out_specs=out_specs,
        out_shape=out_shape,
        scratch_shapes=[pltpu.VMEM((2 * side_rows, depth), jnp.bfloat16)] * 2,
        compiler_params=pltpu.CompilerParams(vmem_limit_bytes=48 * MIB),
        cost_estimate=pl.CostEstimate(
            flops=8 * side_rows * depth * width,
            bytes_accessed=16 * side_rows * depth + 4 * depth * width + 12 * side_rows * width,
            transcendentals=0,
        ),
    )(*blocks, weight, *extra)


def exchange(parts, axis):
    first, third, one_b, three_a, zero_a, zero_b = parts
    lines = one_b.shape[0]
    got1 = swap(first, **{axis: 1})
    got3 = swap(third, **{axis: 3})
    back1 = swap(one_b + got3[:lines], **{axis: 1})
    back3 = swap(three_a + got1[:lines], **{axis: 3})
    return ((zero_a, got1, back3), (zero_b, got3, back1))


def combine_kernel(*refs):
    count = (len(refs) - 6) // 6
    first, third, one_b, three_a, zero_a, zero_b = refs[6 * count :]
    lines = 4 * ROWS
    for chunk in range(count):
        kept_a, got_a, back_a, kept_b, got_b, back_b = refs[6 * chunk : 6 * chunk + 6]
        behind = slice(2 * lines, 3 * lines) if chunk < count - 1 else slice(0, lines)
        here = slice(chunk * ROWS, (chunk + 1) * ROWS)
        later = slice((count + chunk) * ROWS, (count + chunk + 1) * ROWS)
        sum_a = kept_a[...] + got_a[lines : 2 * lines] + back_a[behind]
        sum_b = kept_b[...] + got_b[lines : 2 * lines] + back_b[behind]
        first[here] = sum_a[:ROWS]
        first[later] = sum_a[ROWS : 2 * ROWS]
        zero_a[here] = sum_a[2 * ROWS : 3 * ROWS]
        three_a[here] = sum_a[3 * ROWS :]
        third[here] = sum_b[:ROWS]
        third[later] = sum_b[ROWS : 2 * ROWS]
        zero_b[here] = sum_b[2 * ROWS : 3 * ROWS]
        one_b[here] = sum_b[3 * ROWS :]


def combine(chunks):
    operands = [array for chunk in chunks for side in chunk for array in side]
    count = len(chunks)
    columns = operands[0].shape[1]
    heights = (2 * count, 2 * count, count, count, count, count)
    return pl.pallas_call(
        combine_kernel,
        grid=(columns // TILE,),
        in_specs=[pl.BlockSpec((a.shape[0], TILE), lambda i: (0, i)) for a in operands],
        out_specs=[pl.BlockSpec((h * ROWS, TILE), lambda i: (0, i)) for h in heights],
        out_shape=[jax.ShapeDtypeStruct((h * ROWS, columns), jnp.float32) for h in heights],
        compiler_params=pltpu.CompilerParams(vmem_limit_bytes=56 * MIB),
        cost_estimate=pl.CostEstimate(flops=0, bytes_accessed=12 * MIB, transcendentals=0),
    )(*operands)


def finish_kernel(kept_0, got_0, back_0, kept_1, got_1, back_1, *outs):
    hi = lax.axis_index("head") & 1
    for side, (kept, got, back) in enumerate(((kept_0, got_0, back_0), (kept_1, got_1, back_1))):
        lines = kept.shape[0]
        for request in range(2):
            for way in range(2):
                part = hi ^ way
                row = pl.multiple_of(request * 32 + part * 16, 16)
                later = pl.multiple_of(lines + request * 32 + part * 16, 16)
                outs[2 * way + side][request] = (
                    kept[pl.ds(row, 16), :] + got[pl.ds(later, 16), :] + back[pl.ds(row, 16), :]
                )


def finish(sides):
    columns = sides[0][0].shape[1]
    vmem = pl.BlockSpec(memory_space=pltpu.VMEM)
    return pl.pallas_call(
        finish_kernel,
        in_specs=[vmem] * 6,
        out_specs=[vmem] * 4,
        out_shape=[jax.ShapeDtypeStruct((2, 16, columns), jnp.float32)] * 4,
        compiler_params=pltpu.CompilerParams(vmem_limit_bytes=32 * MIB),
        cost_estimate=pl.CostEstimate(flops=0, bytes_accessed=4 * MIB, transcendentals=0),
    )(*sides[0], *sides[1])


def assemble_kernel(own, near, across, far, mixed):
    _, _, hi, lo, core = place_in_mesh()
    half = own.shape[2] // 2
    for flip, source in enumerate((own, near, across, far)):
        place = (2 * hi + lo) ^ flip
        for side in range(2):
            start = pl.multiple_of((place * 2 + (side ^ core)) * half, half)
            mixed[:, :, pl.ds(start, half)] = source[:, :, side * half : (side + 1) * half]


def assemble(pieces):
    requests, rows, columns = pieces[0].shape
    vmem = pl.BlockSpec(memory_space=pltpu.VMEM)
    return pl.pallas_call(
        assemble_kernel,
        in_specs=[vmem] * 4,
        out_specs=vmem,
        out_shape=jax.ShapeDtypeStruct((requests, rows, 4 * columns), jnp.float32),
        compiler_params=pltpu.CompilerParams(vmem_limit_bytes=32 * MIB),
        cost_estimate=pl.CostEstimate(flops=0, bytes_accessed=2 * MIB, transcendentals=0),
    )(*pieces)


def project(gated, out_weight, w_near):
    lines = 4 * ROWS
    chunks, sent, before = [], [], ()

    def ring(own, *others):
        own = after(own, *others)
        return (own, swap(own, lo=1), swap(own, hi=1, lo=1))

    around = ring(gated[0])
    for at in range(len(gated)):
        own, near, far = around
        opposite = cross(near, far)
        if at == 0:
            w_far = (w_near, swap(after(w_near, near), core=1))
        if at + 1 < len(gated):
            around = ring(gated[at + 1], *((opposite,) if at == 0 else (near, far)))
            if at > 0:
                own = after(own, *around[1:])
        parts = product((own, near, opposite, far), out_weight, w_far, before)
        first, third, one_b, three_a, zero_a, zero_b = parts[:6]
        if at == 0:
            w_far = parts[6]
        got1 = swap(first, first=1)
        got3 = swap(third, first=3)
        before = (got1, got3, one_b, three_a)
        sent.append((zero_a, got1, zero_b, got3))
    got1, got3, one_b, three_a = before
    back1 = swap(one_b + got3[:lines], first=1)
    back3 = swap(three_a + got1[:lines], first=3)
    for at, (zero_a, got1, zero_b, got3) in enumerate(sent):
        if at + 1 < len(sent):
            back_a, back_b = sent[at + 1][3], sent[at + 1][1]
        else:
            back_a, back_b = back3, back1
        chunks.append(((zero_a, got1, back_a), (zero_b, got3, back_b)))
    kept_0, kept_1, away_0, away_1 = finish(exchange(combine(chunks), "second"))
    return assemble(
        (kept_0, swap(kept_1, lo=1), swap(away_0, hi=1), swap(away_1, hi=1, lo=1))
    )


def on_device(
    x_input,
    z_gate,
    bc_input,
    dt_raw,
    a_log,
    d_skip,
    conv_x,
    conv_bc,
    out_weight,
    pool_state,
    pool_xtail,
    pool_bctail,
    pool_dev,
    pool_slot,
    lengths,
):
    outgoing = outgoing_weights(out_weight)
    w_near = swap(outgoing, hi=1, lo=1)
    group = lax.axis_index("head").astype(jnp.uint32) * a_log.shape[0] >> 5
    bc_tail = pool_bctail.reshape(pool_bctail.shape[:2] + (2, GROUPS, STATE))
    bc_tail = lax.dynamic_index_in_dim(bc_tail, group, 3, keepdims=False)
    tails = jnp.concatenate([pool_xtail, bc_tail.reshape(bc_tail.shape[:2] + (2 * STATE,))], axis=-1)
    tails = jnp.pad(tails.astype(jnp.float32), ((0, 0), (5, 0), (0, 0)))
    away_0, away_1, mine, chip, tail_away, tail_mine, tail_chip = prepare(
        pool_dev.reshape(-1), pool_slot, pool_state, after(tails, outgoing)
    )
    tail_near = swap(tail_away, core=1)
    near_0 = swap(after(away_0, tail_away), core=1)
    near_1 = swap(after(away_1, away_0), core=1)
    tail_far = swap(tail_chip + tail_near[:, 1], lo=1)
    tail_rows = tail_mine + tail_near[:, 0] + tail_far
    far_0 = swap(chip[0] + near_0[1], lo=1)
    far_1 = swap(chip[1] + near_1[1], lo=1)
    far_0 = after(far_0, far_1)
    parts = scan(
        lengths, x_input, bc_input, tail_rows, conv_x, conv_bc, dt_raw, a_log, d_skip
    )
    gated, closing = [], []
    for j, (near, far) in enumerate(((near_0, far_0), (near_1, far_1))):
        *rows, state = gate(lengths, j, parts, z_gate, mine, near, far)
        gated += rows
        closing.append(state)
    mixed_out = project(gated, out_weight, w_near)
    return (mixed_out, jnp.concatenate(closing, axis=0))


def solution(mesh):
    return jax.shard_map(
        on_device,
        mesh=mesh,
        in_specs=(
            P("req", None, "head"),
            P("req", None, "head"),
            P("req", None, None),
            P("req", "head", None),
            P("head"),
            P("head"),
            P(None, "head"),
            P(),
            P("head", None),
            P("req", "head", None),
            P("req", None, "head"),
            P("req", None, None),
            P(),
            P(),
            P("req"),
        ),
        out_specs=(P("req", "head", None), P("req", "head", None)),
        check_vma=False,
    )
```

```python
import jax
import jax.numpy as jnp
from jax import lax
from jax.experimental import pallas as pl
from jax.experimental.pallas import tpu as pltpu
from jax.sharding import PartitionSpec as P

HEADS = 256
HEADDIM = 64
STATE = 256
GROUPS = 8
BLOCK = 128
ROWS = (16, 32, 16)
AXES = ("req", "head")
MIB = 1 << 20
VMEM = 60 * MIB


def swap(array, first=0, second=0, hi=0, lo=0, core=0):
    pairs = []
    for source in range(128):
        y, z = (second, first) if source >> 5 & 1 else (first, second)
        pairs.append((source, source ^ (lo << 6 | core << 5 | z << 3 | y << 1 | hi)))
    return lax.ppermute(array, AXES, pairs)


def cross(array):
    pairs = []
    for source in range(128):
        pairs.append((source, source ^ (64 | (source >> 5 & 1))))
    return lax.ppermute(array, AXES, pairs)


def place_in_mesh():
    req, head = lax.axis_index("req"), lax.axis_index("head")
    return head >> 3, head >> 1 & 3, head & 1, req >> 1, req & 1


def conv_rows(window, previous, rows, taps):
    window[0:8, :] = previous
    window[8 : 8 + BLOCK, :] = rows
    total = window[5 : 5 + BLOCK, :] * taps[0:1, :]
    for offset in range(1, 4):
        total = total + window[5 + offset : 5 + offset + BLOCK, :] * taps[offset : offset + 1, :]
    return total * (1.0 / (1.0 + jnp.exp(-total)))


def spread(columns, lane):
    pairs = []
    for pair in range(4):
        even = columns[:, 2 * pair : 2 * pair + 1]
        odd = columns[:, 2 * pair + 1 : 2 * pair + 2]
        pairs.append(jnp.where(lane < HEADDIM, even, odd))
    return jnp.concatenate(pairs, axis=1)


def scan_kernel(
    lengths,
    x_ref,
    b_ref,
    c_ref,
    x_tail,
    b_tail,
    c_tail,
    x_taps,
    b_taps,
    c_taps,
    dt_ref,
    rate_ref,
    skip_ref,
    y_ref,
    c_out,
    decay_out,
    state_out,
    x_window,
    b_window,
    c_window,
    x_last,
    b_last,
    c_last,
    state,
    passed,
):
    request, block = pl.program_id(0), pl.program_id(1)

    @pl.when(block == 0)
    def _():
        x_last[...] = x_tail[0]
        b_last[...] = b_tail[0]
        c_last[...] = c_tail[0]
        state[...] = jnp.zeros_like(state)
        passed[...] = jnp.zeros_like(passed)

    def convolve(window, last, ref, taps):
        rows = ref[0].astype(jnp.float32)
        made = conv_rows(window, last[...], rows, taps[...].astype(jnp.float32))
        last[...] = rows[BLOCK - 8 :]
        return made.astype(jnp.bfloat16)

    x = convolve(x_window, x_last, x_ref, x_taps)
    b = convolve(b_window, b_last, b_ref, b_taps)
    c = convolve(c_window, c_last, c_ref, c_taps)
    c_out[0] = c

    place = lax.broadcasted_iota(jnp.int32, (8, BLOCK), 1)
    raw = dt_ref[0]
    step = jnp.maximum(raw, 0.0) + jnp.log1p(jnp.exp(-jnp.abs(raw)))
    step = jnp.where(place + block * BLOCK < lengths[request], step, 0.0)
    decay = -jnp.exp(rate_ref[...]) * step
    reach = 1
    while reach < BLOCK:
        decay = decay + jnp.where(place >= reach, pltpu.roll(decay, reach, 1), 0.0)
        reach *= 2
    closing = decay[:, BLOCK - 1 : BLOCK]
    weight = jnp.exp(closing - decay) * step
    turned = jnp.transpose(
        jnp.concatenate(
            [decay, weight, passed[...] + decay, jnp.zeros((BLOCK - 24, BLOCK), jnp.float32)],
            axis=0,
        )
    )
    passed[...] = passed[...] + closing
    decay_out[0] = jnp.exp(turned[:, 16:24])

    lane = lax.broadcasted_iota(jnp.int32, (BLOCK, BLOCK), 1)
    causal = lax.broadcasted_iota(jnp.int32, (BLOCK, BLOCK), 0) >= lane
    scores = lax.dot_general(c, b, (((1,), (1,)), ((), ())), preferred_element_type=jnp.float32)
    scores = jnp.where(causal, scores, 0.0)
    within = []
    for pair in range(4):
        inputs = x[:, pair * 128 : (pair + 1) * 128]
        halves = []
        for head in (2 * pair, 2 * pair + 1):
            gap = jnp.where(causal, turned[:, head : head + 1] - decay[head : head + 1, :], 0.0)
            mixing = jnp.exp(gap) * scores * step[head : head + 1, :]
            halves.append(
                jnp.dot(mixing.astype(jnp.bfloat16), inputs, preferred_element_type=jnp.float32)
            )
        within.append(jnp.where(lane < HEADDIM, halves[0], halves[1]))
    carried = lax.dot_general(
        c,
        state[...].astype(jnp.bfloat16),
        (((1,), (1,)), ((), ())),
        preferred_element_type=jnp.float32,
    )
    wide = x.astype(jnp.float32)
    y_ref[0] = (
        jnp.concatenate(within, axis=1)
        + carried * spread(jnp.exp(turned[:, 0:8]), lane)
        + spread(skip_ref[...], lane) * wide
    )
    weighted = (wide * spread(turned[:, 8:16], lane)).astype(jnp.bfloat16)
    added = lax.dot_general(
        weighted, b, (((0,), (0,)), ((), ())), preferred_element_type=jnp.float32
    )
    factor = jnp.exp(closing)
    for head in range(8):
        rows = slice(head * HEADDIM, (head + 1) * HEADDIM)
        state[rows, :] = state[rows, :] * factor[head : head + 1, :] + added[rows, :]

    @pl.when(block == pl.num_programs(1) - 1)
    def _():
        state_out[0] = state[...]


def scan(lengths, x_input, bc_input, tails, conv_x, conv_bc, dt_raw, a_log, d_skip):
    requests, length, width = x_input.shape
    heads = dt_raw.shape[1]

    def group():
        return lax.axis_index("head") * heads >> 5

    def grouped(shift):
        return pl.BlockSpec((1, BLOCK, STATE), lambda r, i: (r, i, group() + shift))

    def table(shift):
        return pl.BlockSpec((4, STATE), lambda r, i: (0, group() + shift))

    def tail(columns, at):
        return pl.BlockSpec((1, 8, columns), lambda r, i: (r, 0, at))

    return pl.pallas_call(
        scan_kernel,
        grid=(requests, length // BLOCK),
        in_specs=[
            pl.BlockSpec(memory_space=pltpu.SMEM),
            pl.BlockSpec((1, BLOCK, width), lambda r, i: (r, i, 0)),
            grouped(0),
            grouped(GROUPS),
            tail(width, 0),
            tail(STATE, width // STATE),
            tail(STATE, width // STATE + 1),
            pl.BlockSpec((4, width), lambda r, i: (0, 0)),
            table(0),
            table(GROUPS),
            pl.BlockSpec((1, heads, BLOCK), lambda r, i: (r, 0, i)),
            pl.BlockSpec((heads, 1), lambda r, i: (0, 0)),
            pl.BlockSpec((1, heads), lambda r, i: (0, 0)),
        ],
        out_specs=[
            pl.BlockSpec((1, BLOCK, width), lambda r, i: (r, i, 0)),
            pl.BlockSpec((1, BLOCK, STATE), lambda r, i: (r, i, 0)),
            pl.BlockSpec((1, BLOCK, heads), lambda r, i: (r, i, 0)),
            pl.BlockSpec((1, width, STATE), lambda r, i: (r, 0, 0)),
        ],
        scratch_shapes=[
            pltpu.VMEM((8 + BLOCK, width), jnp.float32),
            pltpu.VMEM((8 + BLOCK, STATE), jnp.float32),
            pltpu.VMEM((8 + BLOCK, STATE), jnp.float32),
            pltpu.VMEM((8, width), jnp.float32),
            pltpu.VMEM((8, STATE), jnp.float32),
            pltpu.VMEM((8, STATE), jnp.float32),
            pltpu.VMEM((width, STATE), jnp.float32),
            pltpu.VMEM((heads, 1), jnp.float32),
        ],
        out_shape=[
            jax.ShapeDtypeStruct((requests, length, width), jnp.float32),
            jax.ShapeDtypeStruct((requests, length, STATE), jnp.bfloat16),
            jax.ShapeDtypeStruct((requests, length, heads), jnp.float32),
            jax.ShapeDtypeStruct((requests, width, STATE), jnp.float32),
        ],
        compiler_params=pltpu.CompilerParams(vmem_limit_bytes=VMEM),
        cost_estimate=pl.CostEstimate(
            flops=2 * requests * length * (8 * 128 * 128 + 2 * width * STATE + 128 * STATE),
            bytes_accessed=12 * MIB,
            transcendentals=4 * requests * length * width,
        ),
    )(
        lengths,
        x_input,
        bc_input,
        bc_input,
        tails,
        tails,
        tails,
        conv_x,
        conv_bc,
        conv_bc,
        dt_raw,
        a_log[:, None],
        d_skip[None, :],
    )


def outgoing_kernel(weight, outgoing, columns, semaphore):
    _, _, hi, lo, core = place_in_mesh()
    half = columns.shape[1]
    start = pl.multiple_of(((3 - 2 * hi - lo) * 2 + core) * half, half)
    copy = pltpu.make_async_copy(weight.at[:, pl.ds(start, half)], columns, semaphore)
    copy.start()
    copy.wait()
    outgoing[...] = columns[...].astype(jnp.float32)


def outgoing_weights(weight):
    half = weight.shape[1] // 8
    return pl.pallas_call(
        outgoing_kernel,
        in_specs=[pl.BlockSpec(memory_space=pl.ANY)],
        out_specs=pl.BlockSpec(memory_space=pltpu.VMEM),
        out_shape=jax.ShapeDtypeStruct((weight.shape[0], half), jnp.float32),
        scratch_shapes=[
            pltpu.VMEM((weight.shape[0], half), weight.dtype),
            pltpu.SemaphoreType.DMA,
        ],
        compiler_params=pltpu.CompilerParams(vmem_limit_bytes=VMEM),
        cost_estimate=pl.CostEstimate(flops=0, bytes_accessed=3 * MIB, transcendentals=0),
    )(weight)


def prepare_kernel(
    owner, slot, pool, tails, _, away_0, away_1, mine, chip, tail_away, tail_mine, tail_chip
):
    _, _, _, lo, core = place_in_mesh()
    me = 2 * lo + core
    for j in range(2):
        away = (away_0, away_1)[j]
        for device, state, tail in (
            (me ^ 1, away.at[0], tail_away.at[j, 0]),
            (me ^ 3, away.at[1], tail_away.at[j, 1]),
            (me ^ 2, chip.at[j], tail_chip.at[j]),
            (me, mine.at[j], tail_mine.at[j]),
        ):
            request = 2 * device + j
            here = owner[request] == me
            at = slot[request]
            state[...] = jnp.where(here, pool[at], 0.0)
            tail[...] = jnp.where(here, tails[at], 0.0)


def prepare(owner, slot, pool, tails, outgoing):
    _, width, state = pool.shape
    columns = tails.shape[2]
    vmem = pl.BlockSpec(memory_space=pltpu.VMEM)
    smem = pl.BlockSpec(memory_space=pltpu.SMEM)
    shapes = (
        (2, width, state),
        (2, width, state),
        (2, width, state),
        (2, width, state),
        (2, 2, 8, columns),
        (2, 8, columns),
        (2, 8, columns),
    )
    return pl.pallas_call(
        prepare_kernel,
        in_specs=[smem, smem, vmem, vmem, pl.BlockSpec(memory_space=pl.ANY)],
        out_specs=[vmem] * len(shapes),
        out_shape=[jax.ShapeDtypeStruct(s, jnp.float32) for s in shapes],
        compiler_params=pltpu.CompilerParams(vmem_limit_bytes=VMEM),
        cost_estimate=pl.CostEstimate(flops=0, bytes_accessed=7 * MIB, transcendentals=0),
    )(owner, slot, pool, tails, outgoing)


def gate_kernel(
    lengths, y_ref, c_ref, decay_ref, part_ref, z_ref, mine, near_0, near_1, far_0, far_1, *outs
):
    z_at, y_at, _, _, core = place_in_mesh()
    chunks, state_ref = outs[:3], outs[3]
    lane = lax.broadcasted_iota(jnp.int32, (BLOCK, BLOCK), 1)
    length = y_ref.shape[1]
    homes = (((0, 0), (1, 0)), ((1, 16), (2, 0)))
    for request, (near, far) in enumerate(((near_0, far_0), (near_1, far_1))):
        initial = mine[request] + near[0] + far[...]
        narrow = initial.astype(jnp.bfloat16)
        for block in range(length // BLOCK):
            rows = slice(block * BLOCK, (block + 1) * BLOCK)
            carried = lax.dot_general(
                c_ref[request, rows],
                narrow,
                (((1,), (1,)), ((), ())),
                preferred_element_type=jnp.float32,
            )
            y = y_ref[request, rows] + carried * spread(decay_ref[request, rows], lane)
            z = z_ref[request, rows].astype(jnp.float32)
            position = lax.broadcasted_iota(jnp.int32, y.shape, 0) + block * BLOCK
            gated = y * (z * (1.0 / (1.0 + jnp.exp(-z))))
            gated = jnp.where(position < lengths[request], gated, 0.0)
            gated = gated.astype(jnp.bfloat16).astype(jnp.float32)
            for at in range(4):
                z_far, y_far = block ^ z_at, at ^ y_at
                cell = jnp.where(core == 0, y_far * 4 + z_far, z_far * 4 + y_far)
                for part, (chunk, offset) in enumerate(homes[request]):
                    for hi in range(2):
                        start = at * 32 + hi * 16 + part * 8
                        target = pl.multiple_of(cell * ROWS[chunk] + offset + hi * 8, 8)
                        chunks[chunk][pl.ds(target, 8), :] = gated[start : start + 8]
        final = decay_ref[request, length - 8 :, :]
        for head in range(8):
            rows = slice(head * HEADDIM, (head + 1) * HEADDIM)
            state_ref[request, rows] = (
                part_ref[request, rows] + initial[rows] * final[7:8, head : head + 1]
            )


def gate(lengths, parts, z_gate, *states):
    y, c, decay, part = parts
    requests, length, width = y.shape
    vmem = pl.BlockSpec(memory_space=pltpu.VMEM)
    return pl.pallas_call(
        gate_kernel,
        in_specs=[pl.BlockSpec(memory_space=pltpu.SMEM)] + [vmem] * 10,
        out_specs=[vmem] * 4,
        out_shape=[jax.ShapeDtypeStruct((16 * rows, width), jnp.float32) for rows in ROWS]
        + [jax.ShapeDtypeStruct(part.shape, jnp.float32)],
        compiler_params=pltpu.CompilerParams(vmem_limit_bytes=VMEM),
        cost_estimate=pl.CostEstimate(
            flops=4 * length * width * STATE, bytes_accessed=12 * MIB, transcendentals=0
        ),
    )(lengths, y, c, decay, part, z_gate, *states)


def hold(array, *others):
    anywhere = pl.BlockSpec(memory_space=pl.ANY)

    def kernel(*refs):
        pass

    return pl.pallas_call(
        kernel,
        in_specs=[anywhere] * (1 + len(others)),
        out_specs=anywhere,
        out_shape=jax.ShapeDtypeStruct(array.shape, array.dtype),
        input_output_aliases={0: 0},
        compiler_params=pltpu.CompilerParams(vmem_limit_bytes=VMEM),
        cost_estimate=pl.CostEstimate(flops=0, bytes_accessed=0, transcendentals=0),
    )(array, *others)


def choose(near, far, *others):
    rows, columns = near.shape
    tile = pl.BlockSpec((rows, 128), lambda i: (0, i))

    def kernel(near_ref, far_ref, *refs):
        core = lax.axis_index("req") & 1
        refs[-1][...] = jnp.where(core == 0, far_ref[...], near_ref[...])

    return pl.pallas_call(
        kernel,
        grid=(columns // 128,),
        in_specs=[tile] * 2 + [pl.BlockSpec(memory_space=pl.ANY)] * len(others),
        out_specs=tile,
        out_shape=jax.ShapeDtypeStruct(near.shape, near.dtype),
        compiler_params=pltpu.CompilerParams(vmem_limit_bytes=VMEM),
        cost_estimate=pl.CostEstimate(flops=0, bytes_accessed=3 * MIB, transcendentals=0),
    )(near, far, *others)


ORDER = ((2, 1, 0, 3), (2, 3, 0, 1))
TILE = 512


SENT = ((2, 1), (2, 3))
KEPT = ((3, 0), (1, 0))


def product(blocks, majors, weight, w_far, others):
    depth = weight.shape[0]
    width = weight.shape[1] // 4
    rows = blocks[0].shape[0] // 16
    lines = 4 * rows
    tiles = width // (2 * TILE)
    opening = isinstance(w_far, tuple)
    join = majors is SENT
    heights = (2 * lines, 2 * lines) if join else (lines,) * 4

    def kernel(*refs):
        own, near, opposite, far, w_own_ref = refs[:5]
        outs, own_side, far_side = refs[-2 - opening - len(heights) : -2], refs[-2], refs[-1]
        step = pl.program_id(0)

        @pl.when(step == 0)
        def _():
            at = 0
            for side, (own_ref, far_ref) in enumerate(((own, opposite), (near, far))):
                for major in majors[side]:
                    span = slice(major * lines, (major + 1) * lines)
                    own_side[at : at + lines] = own_ref[span].astype(jnp.bfloat16)
                    far_side[at : at + lines] = far_ref[span].astype(jnp.bfloat16)
                    at += lines

        if opening:
            far_weight = outs[len(heights)]

            @pl.when(step < tiles)
            def _():
                far_weight[...] = refs[5][...].astype(jnp.bfloat16)

            @pl.when(step >= tiles)
            def _():
                far_weight[...] = refs[6][...].astype(jnp.bfloat16)
        else:
            far_weight = refs[5]

        total = jnp.dot(own_side[...], w_own_ref[...], preferred_element_type=jnp.float32)
        total += jnp.dot(far_side[...], far_weight[...], preferred_element_type=jnp.float32)
        for side in range(2):
            for which in range(2):
                ref = outs[side] if join else outs[2 * side + which]
                for at, minor in enumerate(ORDER[side]):
                    to = (join * which * 4 + at) * rows
                    start = (side * 2 + which) * lines + minor * rows
                    ref[to : to + rows, :] = total[start : start + rows]

    def own_columns(i):
        _, _, hi, lo, core = place_in_mesh()
        side = jnp.where(i < tiles, core, 1 - core)
        return (0, ((2 * hi + lo) * 2 + side) * tiles + jnp.where(i < tiles, i, i - tiles))

    def tile(rows):
        return pl.BlockSpec((rows, TILE), lambda i: (0, i))

    if opening:
        extra_specs = [
            pl.BlockSpec((depth, TILE), lambda i: (0, jnp.minimum(i, tiles - 1))),
            pl.BlockSpec((depth, TILE), lambda i: (0, jnp.maximum(i - tiles, 0))),
        ]
        extra = w_far
    else:
        extra_specs = [tile(depth)]
        extra = (w_far,)
    out_specs = [tile(h) for h in heights]
    out_shape = [jax.ShapeDtypeStruct((h, width), jnp.float32) for h in heights]
    if opening:
        out_specs.append(tile(depth))
        out_shape.append(jax.ShapeDtypeStruct((depth, width), jnp.bfloat16))
    return pl.pallas_call(
        kernel,
        grid=(2 * tiles,),
        in_specs=[pl.BlockSpec(b.shape, lambda i: (0, 0)) for b in blocks]
        + [pl.BlockSpec((depth, TILE), own_columns)]
        + extra_specs
        + [pl.BlockSpec(memory_space=pl.ANY)] * len(others),
        out_specs=out_specs,
        out_shape=out_shape,
        scratch_shapes=[pltpu.VMEM((4 * lines, depth), jnp.bfloat16)] * 2,
        compiler_params=pltpu.CompilerParams(vmem_limit_bytes=VMEM),
        cost_estimate=pl.CostEstimate(
            flops=16 * lines * depth * width,
            bytes_accessed=16 * lines * depth + 4 * depth * width + 16 * lines * width,
            transcendentals=0,
        ),
    )(*blocks, weight, *extra, *others)


def relay(one_b, three_a, got1, got3, *others):
    lines, columns = one_b.shape
    tile = pl.BlockSpec((lines, columns // 2), lambda i: (0, i))

    def kernel(*refs):
        one_ref, three_ref, got1_ref, got3_ref = refs[:4]
        refs[-2][...] = one_ref[...] + got3_ref[...]
        refs[-1][...] = three_ref[...] + got1_ref[...]

    return pl.pallas_call(
        kernel,
        grid=(2,),
        in_specs=[tile] * 4 + [pl.BlockSpec(memory_space=pl.ANY)] * len(others),
        out_specs=[tile] * 2,
        out_shape=[jax.ShapeDtypeStruct((lines, columns), jnp.float32)] * 2,
        compiler_params=pltpu.CompilerParams(vmem_limit_bytes=VMEM),
        cost_estimate=pl.CostEstimate(
            flops=0, bytes_accessed=24 * lines * columns, transcendentals=0
        ),
    )(one_b, three_a, got1, got3, *others)


def combine(chunks, *others):
    operands, specs, heights = [], [], []
    for chunk in chunks:
        lines, columns = chunk[0].shape
        heights.append(lines // 4)
        for place, array in enumerate(chunk):
            operands.append(array)
            specs.append(pl.BlockSpec((lines, TILE), lambda i, at=place % 3 == 1: (int(at), i)))
    total = sum(heights)

    def kernel(*refs):
        first, third, one_b, three_a, zero_a, zero_b = refs[-6:]
        here = 0
        for chunk, rows in enumerate(heights):
            kept_a, got_a, back_a, kept_b, got_b, back_b = refs[6 * chunk : 6 * chunk + 6]
            sum_a = kept_a[...] + got_a[...] + back_a[...]
            sum_b = kept_b[...] + got_b[...] + back_b[...]
            for ref, summed, minor, start in (
                (first, sum_a, 0, here),
                (first, sum_a, 1, total + here),
                (zero_a, sum_a, 2, here),
                (three_a, sum_a, 3, here),
                (third, sum_b, 0, here),
                (third, sum_b, 1, total + here),
                (zero_b, sum_b, 2, here),
                (one_b, sum_b, 3, here),
            ):
                ref[start : start + rows] = summed[minor * rows : (minor + 1) * rows]
            here += rows

    made = (2 * total, 2 * total, total, total, total, total)
    return pl.pallas_call(
        kernel,
        grid=(columns // TILE,),
        in_specs=specs + [pl.BlockSpec(memory_space=pl.ANY)] * len(others),
        out_specs=[pl.BlockSpec((h, TILE), lambda i: (0, i)) for h in made],
        out_shape=[jax.ShapeDtypeStruct((h, columns), jnp.float32) for h in made],
        compiler_params=pltpu.CompilerParams(vmem_limit_bytes=VMEM),
        cost_estimate=pl.CostEstimate(
            flops=0, bytes_accessed=128 * total * columns, transcendentals=0
        ),
    )(*operands, *others)


def finish_kernel(*refs):
    hi = lax.axis_index("head") & 1
    outs = refs[12:]
    for side in range(2):
        for way in range(2):
            to = 0
            for part in range(2):
                kept, got, back = refs[6 * part + 3 * side : 6 * part + 3 * side + 3]
                lines = kept.shape[0]
                for block in range(lines // 16):
                    row = pl.multiple_of(block * 16 + (hi ^ way) * 8, 8)
                    later = pl.multiple_of(lines + row, 8)
                    outs[2 * way + side][to : to + 8, :] = (
                        kept[pl.ds(row, 8), :] + got[pl.ds(later, 8), :] + back[pl.ds(row, 8), :]
                    )
                    to += 8


def finish(*terms):
    columns = terms[0].shape[1]
    vmem = pl.BlockSpec(memory_space=pltpu.VMEM)
    return pl.pallas_call(
        finish_kernel,
        in_specs=[vmem] * 12,
        out_specs=[vmem] * 4,
        out_shape=[jax.ShapeDtypeStruct((32, columns), jnp.float32)] * 4,
        compiler_params=pltpu.CompilerParams(vmem_limit_bytes=VMEM),
        cost_estimate=pl.CostEstimate(flops=0, bytes_accessed=4 * MIB, transcendentals=0),
    )(*terms)


def assemble_kernel(own, near, across, far, mixed):
    _, _, hi, lo, core = place_in_mesh()
    half = own.shape[1] // 2
    for flip, source in enumerate((own, near, across, far)):
        place = (2 * hi + lo) ^ flip
        for side in range(2):
            start = pl.multiple_of((place * 2 + (side ^ core)) * half, half)
            for request in range(2):
                mixed[request, :, pl.ds(start, half)] = source[
                    request * 16 : request * 16 + 16, side * half : (side + 1) * half
                ]


def assemble(pieces):
    rows, columns = pieces[0].shape
    vmem = pl.BlockSpec(memory_space=pltpu.VMEM)
    return pl.pallas_call(
        assemble_kernel,
        in_specs=[vmem] * 4,
        out_specs=vmem,
        out_shape=jax.ShapeDtypeStruct((2, rows // 2, 4 * columns), jnp.float32),
        compiler_params=pltpu.CompilerParams(vmem_limit_bytes=VMEM),
        cost_estimate=pl.CostEstimate(flops=0, bytes_accessed=2 * MIB, transcendentals=0),
    )(*pieces)


def project(gated, out_weight, w_near):
    def ring(own):
        return (own, swap(own, lo=1), swap(own, hi=1, lo=1))

    def first_round(parts, axis):
        return (swap(parts[0], **{axis: 1}), swap(parts[1], **{axis: 3}))

    def second_round(parts, got, axis, *others):
        sent = relay(parts[2], parts[3], *got, *others)
        return (swap(sent[0], **{axis: 1}), swap(sent[1], **{axis: 3})), sent[0]

    def multiply(blocks, w_far, *others):
        sent = product(blocks, SENT, out_weight, w_far, others)
        w_far = sent[2] if isinstance(w_far, tuple) else w_far
        three_a, zero_a, one_b, zero_b = product(blocks, KEPT, out_weight, w_far, (sent[0],))
        return (sent[0], sent[1], one_b, three_a, zero_a, zero_b), w_far

    def terms(parts, got, back):
        return (parts[4], got[0], back[1], parts[5], got[1], back[0])

    own, near, far = ring(gated[0])
    chosen = choose(near, far)
    w_near = hold(w_near, chosen)
    w_far = (w_near, swap(w_near, core=1))
    opposite = cross(chosen)
    blocks = (own, near, opposite, far)
    own, near, far = ring(hold(gated[1], opposite))
    parts_0, w_far = multiply(blocks, w_far)
    got_0 = first_round(parts_0, "first")

    chosen = choose(near, far, parts_0[4])
    opposite = cross(chosen)
    blocks = (own, near, opposite, far)
    back_0, token = second_round(parts_0, got_0, "first", chosen)
    own, near, far = ring(hold(gated[2], opposite, token))
    parts_1, _ = multiply(blocks, w_far, back_0[0], back_0[1])
    got_1 = first_round(parts_1, "first")

    chosen = choose(near, far, parts_1[4])
    blocks = (own, near, cross(chosen), far)
    back_1, token = second_round(parts_1, got_1, "first", chosen)
    parts_2, _ = multiply(blocks, w_far, token)
    got_2 = first_round(parts_2, "first")

    later_a = combine([terms(parts_0, got_0, back_0), terms(parts_1, got_1, back_1)], parts_2[4])
    over_a = first_round(later_a, "second")
    back_2, token = second_round(parts_2, got_2, "first", later_a[4])
    last_a, token = second_round(later_a, over_a, "second", token)
    later_b = combine([terms(parts_2, got_2, back_2)], token)
    over_b = first_round(later_b, "second")
    last_b, _ = second_round(later_b, over_b, "second")
    kept_0, kept_1, away_0, away_1 = finish(
        *terms(later_a, over_a, last_a), *terms(later_b, over_b, last_b)
    )
    return assemble(
        (kept_0, swap(kept_1, lo=1), swap(away_0, hi=1), swap(away_1, hi=1, lo=1))
    )


def on_device(
    x_input,
    z_gate,
    bc_input,
    dt_raw,
    a_log,
    d_skip,
    conv_x,
    conv_bc,
    out_weight,
    pool_state,
    pool_xtail,
    pool_bctail,
    pool_dev,
    pool_slot,
    lengths,
):
    outgoing = outgoing_weights(out_weight)
    w_near = swap(outgoing, hi=1, lo=1)
    group = lax.axis_index("head").astype(jnp.uint32) * a_log.shape[0] >> 5
    bc_tail = pool_bctail.reshape(pool_bctail.shape[:2] + (2, GROUPS, STATE))
    bc_tail = lax.dynamic_index_in_dim(bc_tail, group, 3, keepdims=False)
    tails = jnp.concatenate([pool_xtail, bc_tail.reshape(bc_tail.shape[:2] + (2 * STATE,))], axis=-1)
    tails = jnp.pad(tails.astype(jnp.float32), ((0, 0), (5, 0), (0, 0)))
    away_0, away_1, mine, chip, tail_away, tail_mine, tail_chip = prepare(
        pool_dev.reshape(-1), pool_slot, pool_state, tails, outgoing
    )
    tail_near = swap(tail_away, core=1)
    near_0 = swap(away_0, core=1)
    near_1 = swap(away_1, core=1)
    tail_far = swap(tail_chip + tail_near[:, 1], lo=1)
    chip = hold(chip, tail_far)
    tail_rows = tail_mine + tail_near[:, 0] + tail_far
    far_0 = swap(chip[0] + near_0[1], lo=1)
    far_1 = swap(chip[1] + near_1[1], lo=1)
    parts = scan(
        lengths, x_input, bc_input, tail_rows, conv_x, conv_bc, dt_raw, a_log, d_skip
    )
    *gated, final_state = gate(lengths, parts, z_gate, mine, near_0, near_1, far_0, far_1)
    mixed_out = project(gated, out_weight, w_near)
    return (mixed_out, final_state)


def solution(mesh):
    return jax.shard_map(
        on_device,
        mesh=mesh,
        in_specs=(
            P("req", None, "head"),
            P("req", None, "head"),
            P("req", None, None),
            P("req", "head", None),
            P("head"),
            P("head"),
            P(None, "head"),
            P(),
            P("head", None),
            P("req", "head", None),
            P("req", None, "head"),
            P("req", None, None),
            P(),
            P(),
            P("req"),
        ),
        out_specs=(P("req", "head", None), P("req", "head", None)),
        check_vma=False,
    )
```

```python
import jax
import jax.numpy as jnp
from jax import lax
from jax.experimental import pallas as pl
from jax.experimental.pallas import tpu as pltpu
from jax.sharding import PartitionSpec as P

HEADS = 256
HEADDIM = 64
STATE = 256
GROUPS = 8
BLOCK = 128
ROWS = (16, 32, 16)
AXES = ("req", "head")
MIB = 1 << 20
VMEM = 60 * MIB


def swap(array, first=0, second=0, hi=0, lo=0, core=0):
    pairs = []
    for source in range(128):
        y, z = (second, first) if source >> 5 & 1 else (first, second)
        pairs.append((source, source ^ (lo << 6 | core << 5 | z << 3 | y << 1 | hi)))
    return lax.ppermute(array, AXES, pairs)


def cross(array):
    pairs = []
    for source in range(128):
        pairs.append((source, source ^ (64 | (source >> 5 & 1))))
    return lax.ppermute(array, AXES, pairs)


def place_in_mesh():
    req, head = lax.axis_index("req"), lax.axis_index("head")
    return head >> 3, head >> 1 & 3, head & 1, req >> 1, req & 1


def conv_rows(window, previous, rows, taps):
    window[0:8, :] = previous
    window[8 : 8 + BLOCK, :] = rows
    total = window[5 : 5 + BLOCK, :] * taps[0:1, :]
    for offset in range(1, 4):
        total = total + window[5 + offset : 5 + offset + BLOCK, :] * taps[offset : offset + 1, :]
    return total * (1.0 / (1.0 + jnp.exp(-total)))


def spread(columns, lane):
    pairs = []
    for pair in range(4):
        even = columns[:, 2 * pair : 2 * pair + 1]
        odd = columns[:, 2 * pair + 1 : 2 * pair + 2]
        pairs.append(jnp.where(lane < HEADDIM, even, odd))
    return jnp.concatenate(pairs, axis=1)


def scan_kernel(
    lengths,
    x_ref,
    b_ref,
    c_ref,
    x_tail,
    b_tail,
    c_tail,
    x_taps,
    b_taps,
    c_taps,
    dt_ref,
    rate_ref,
    skip_ref,
    y_ref,
    c_out,
    decay_out,
    state_out,
    x_window,
    b_window,
    c_window,
    x_last,
    b_last,
    c_last,
    state,
    passed,
):
    request, block = pl.program_id(0), pl.program_id(1)

    @pl.when(block == 0)
    def _():
        x_last[...] = x_tail[0]
        b_last[...] = b_tail[0]
        c_last[...] = c_tail[0]
        state[...] = jnp.zeros_like(state)
        passed[...] = jnp.zeros_like(passed)

    def convolve(window, last, ref, taps):
        rows = ref[0].astype(jnp.float32)
        made = conv_rows(window, last[...], rows, taps[...].astype(jnp.float32))
        last[...] = rows[BLOCK - 8 :]
        return made.astype(jnp.bfloat16)

    x = convolve(x_window, x_last, x_ref, x_taps)
    b = convolve(b_window, b_last, b_ref, b_taps)
    c = convolve(c_window, c_last, c_ref, c_taps)
    c_out[0] = c

    place = lax.broadcasted_iota(jnp.int32, (8, BLOCK), 1)
    raw = dt_ref[0]
    step = jnp.maximum(raw, 0.0) + jnp.log1p(jnp.exp(-jnp.abs(raw)))
    step = jnp.where(place + block * BLOCK < lengths[request], step, 0.0)
    decay = -jnp.exp(rate_ref[...]) * step
    reach = 1
    while reach < BLOCK:
        decay = decay + jnp.where(place >= reach, pltpu.roll(decay, reach, 1), 0.0)
        reach *= 2
    closing = decay[:, BLOCK - 1 : BLOCK]
    weight = jnp.exp(closing - decay) * step
    turned = jnp.transpose(
        jnp.concatenate(
            [decay, weight, passed[...] + decay, jnp.zeros((BLOCK - 24, BLOCK), jnp.float32)],
            axis=0,
        )
    )
    passed[...] = passed[...] + closing
    decay_out[0] = jnp.exp(turned[:, 16:24])

    lane = lax.broadcasted_iota(jnp.int32, (BLOCK, BLOCK), 1)
    causal = lax.broadcasted_iota(jnp.int32, (BLOCK, BLOCK), 0) >= lane
    scores = lax.dot_general(c, b, (((1,), (1,)), ((), ())), preferred_element_type=jnp.float32)
    scores = jnp.where(causal, scores, 0.0)
    within = []
    for pair in range(4):
        inputs = x[:, pair * 128 : (pair + 1) * 128]
        halves = []
        for head in (2 * pair, 2 * pair + 1):
            gap = jnp.where(causal, turned[:, head : head + 1] - decay[head : head + 1, :], 0.0)
            mixing = jnp.exp(gap) * scores * step[head : head + 1, :]
            halves.append(
                jnp.dot(mixing.astype(jnp.bfloat16), inputs, preferred_element_type=jnp.float32)
            )
        within.append(jnp.where(lane < HEADDIM, halves[0], halves[1]))
    carried = lax.dot_general(
        c,
        state[...].astype(jnp.bfloat16),
        (((1,), (1,)), ((), ())),
        preferred_element_type=jnp.float32,
    )
    wide = x.astype(jnp.float32)
    y_ref[0] = (
        jnp.concatenate(within, axis=1)
        + carried * spread(jnp.exp(turned[:, 0:8]), lane)
        + spread(skip_ref[...], lane) * wide
    )
    weighted = (wide * spread(turned[:, 8:16], lane)).astype(jnp.bfloat16)
    added = lax.dot_general(
        weighted, b, (((0,), (0,)), ((), ())), preferred_element_type=jnp.float32
    )
    factor = jnp.exp(closing)
    for head in range(8):
        rows = slice(head * HEADDIM, (head + 1) * HEADDIM)
        state[rows, :] = state[rows, :] * factor[head : head + 1, :] + added[rows, :]

    @pl.when(block == pl.num_programs(1) - 1)
    def _():
        state_out[0] = state[...]


def scan(lengths, x_input, bc_input, tails, conv_x, conv_bc, dt_raw, a_log, d_skip):
    requests, length, width = x_input.shape
    heads = dt_raw.shape[1]

    def group():
        return lax.axis_index("head") * heads >> 5

    def grouped(shift):
        return pl.BlockSpec((1, BLOCK, STATE), lambda r, i: (r, i, group() + shift))

    def table(shift):
        return pl.BlockSpec((4, STATE), lambda r, i: (0, group() + shift))

    def tail(columns, at):
        return pl.BlockSpec((1, 8, columns), lambda r, i: (r, 0, at))

    return pl.pallas_call(
        scan_kernel,
        grid=(requests, length // BLOCK),
        in_specs=[
            pl.BlockSpec(memory_space=pltpu.SMEM),
            pl.BlockSpec((1, BLOCK, width), lambda r, i: (r, i, 0)),
            grouped(0),
            grouped(GROUPS),
            tail(width, 0),
            tail(STATE, width // STATE),
            tail(STATE, width // STATE + 1),
            pl.BlockSpec((4, width), lambda r, i: (0, 0)),
            table(0),
            table(GROUPS),
            pl.BlockSpec((1, heads, BLOCK), lambda r, i: (r, 0, i)),
            pl.BlockSpec((heads, 1), lambda r, i: (0, 0)),
            pl.BlockSpec((1, heads), lambda r, i: (0, 0)),
        ],
        out_specs=[
            pl.BlockSpec((1, BLOCK, width), lambda r, i: (r, i, 0)),
            pl.BlockSpec((1, BLOCK, STATE), lambda r, i: (r, i, 0)),
            pl.BlockSpec((1, BLOCK, heads), lambda r, i: (r, i, 0)),
            pl.BlockSpec((1, width, STATE), lambda r, i: (r, 0, 0)),
        ],
        scratch_shapes=[
            pltpu.VMEM((8 + BLOCK, width), jnp.float32),
            pltpu.VMEM((8 + BLOCK, STATE), jnp.float32),
            pltpu.VMEM((8 + BLOCK, STATE), jnp.float32),
            pltpu.VMEM((8, width), jnp.float32),
            pltpu.VMEM((8, STATE), jnp.float32),
            pltpu.VMEM((8, STATE), jnp.float32),
            pltpu.VMEM((width, STATE), jnp.float32),
            pltpu.VMEM((heads, 1), jnp.float32),
        ],
        out_shape=[
            jax.ShapeDtypeStruct((requests, length, width), jnp.float32),
            jax.ShapeDtypeStruct((requests, length, STATE), jnp.bfloat16),
            jax.ShapeDtypeStruct((requests, length, heads), jnp.float32),
            jax.ShapeDtypeStruct((requests, width, STATE), jnp.float32),
        ],
        compiler_params=pltpu.CompilerParams(vmem_limit_bytes=VMEM),
        cost_estimate=pl.CostEstimate(
            flops=2 * requests * length * (8 * 128 * 128 + 2 * width * STATE + 128 * STATE),
            bytes_accessed=12 * MIB,
            transcendentals=4 * requests * length * width,
        ),
    )(
        lengths,
        x_input,
        bc_input,
        bc_input,
        tails,
        tails,
        tails,
        conv_x,
        conv_bc,
        conv_bc,
        dt_raw,
        a_log[:, None],
        d_skip[None, :],
    )


def prepare_kernel(
    owner,
    slot,
    pool,
    tails,
    weight,
    away_0,
    away_1,
    mine,
    chip,
    tail_away,
    tail_mine,
    tail_chip,
    outgoing,
    columns,
    semaphore,
):
    _, _, hi, lo, core = place_in_mesh()
    half = columns.shape[1]
    start = pl.multiple_of(((3 - 2 * hi - lo) * 2 + core) * half, half)
    copy = pltpu.make_async_copy(weight.at[:, pl.ds(start, half)], columns, semaphore)
    copy.start()
    me = 2 * lo + core
    for j in range(2):
        away = (away_0, away_1)[j]
        for device, state, tail in (
            (me ^ 1, away.at[0], tail_away.at[j, 0]),
            (me ^ 3, away.at[1], tail_away.at[j, 1]),
            (me ^ 2, chip.at[j], tail_chip.at[j]),
            (me, mine.at[j], tail_mine.at[j]),
        ):
            request = 2 * device + j
            here = owner[request] == me
            at = slot[request]
            state[...] = jnp.where(here, pool[at], 0.0)
            tail[...] = jnp.where(here, tails[at], 0.0)
    copy.wait()
    outgoing[...] = columns[...].astype(jnp.float32)


def prepare(owner, slot, pool, tails, weight):
    _, width, state = pool.shape
    half = weight.shape[1] // 8
    columns = tails.shape[2]
    vmem = pl.BlockSpec(memory_space=pltpu.VMEM)
    smem = pl.BlockSpec(memory_space=pltpu.SMEM)
    shapes = (
        (2, width, state),
        (2, width, state),
        (2, width, state),
        (2, width, state),
        (2, 2, 8, columns),
        (2, 8, columns),
        (2, 8, columns),
        (weight.shape[0], half),
    )
    return pl.pallas_call(
        prepare_kernel,
        in_specs=[smem, smem, vmem, vmem, pl.BlockSpec(memory_space=pl.ANY)],
        out_specs=[vmem] * len(shapes),
        out_shape=[jax.ShapeDtypeStruct(s, jnp.float32) for s in shapes],
        scratch_shapes=[
            pltpu.VMEM((weight.shape[0], half), weight.dtype),
            pltpu.SemaphoreType.DMA,
        ],
        compiler_params=pltpu.CompilerParams(vmem_limit_bytes=VMEM),
        cost_estimate=pl.CostEstimate(flops=0, bytes_accessed=7 * MIB, transcendentals=0),
    )(owner, slot, pool, tails, weight)


def gate_kernel(
    lengths, y_ref, c_ref, decay_ref, part_ref, z_ref, mine, near_0, near_1, far_0, far_1, *outs
):
    z_at, y_at, _, _, core = place_in_mesh()
    chunks, state_ref = outs[:3], outs[3]
    lane = lax.broadcasted_iota(jnp.int32, (BLOCK, BLOCK), 1)
    length = y_ref.shape[1]
    homes = (((0, 0), (1, 0)), ((1, 16), (2, 0)))
    for request, (near, far) in enumerate(((near_0, far_0), (near_1, far_1))):
        initial = mine[request] + near[0] + far[...]
        narrow = initial.astype(jnp.bfloat16)
        for block in range(length // BLOCK):
            rows = slice(block * BLOCK, (block + 1) * BLOCK)
            carried = lax.dot_general(
                c_ref[request, rows],
                narrow,
                (((1,), (1,)), ((), ())),
                preferred_element_type=jnp.float32,
            )
            y = y_ref[request, rows] + carried * spread(decay_ref[request, rows], lane)
            z = z_ref[request, rows].astype(jnp.float32)
            position = lax.broadcasted_iota(jnp.int32, y.shape, 0) + block * BLOCK
            gated = y * (z * (1.0 / (1.0 + jnp.exp(-z))))
            gated = jnp.where(position < lengths[request], gated, 0.0)
            gated = gated.astype(jnp.bfloat16).astype(jnp.float32)
            for at in range(4):
                z_far, y_far = block ^ z_at, at ^ y_at
                cell = jnp.where(core == 0, y_far * 4 + z_far, z_far * 4 + y_far)
                for part, (chunk, offset) in enumerate(homes[request]):
                    for hi in range(2):
                        start = at * 32 + hi * 16 + part * 8
                        target = pl.multiple_of(cell * ROWS[chunk] + offset + hi * 8, 8)
                        chunks[chunk][pl.ds(target, 8), :] = gated[start : start + 8]
        final = decay_ref[request, length - 8 :, :]
        for head in range(8):
            rows = slice(head * HEADDIM, (head + 1) * HEADDIM)
            state_ref[request, rows] = (
                part_ref[request, rows] + initial[rows] * final[7:8, head : head + 1]
            )


def gate(lengths, parts, z_gate, *states):
    y, c, decay, part = parts
    requests, length, width = y.shape
    vmem = pl.BlockSpec(memory_space=pltpu.VMEM)
    return pl.pallas_call(
        gate_kernel,
        in_specs=[pl.BlockSpec(memory_space=pltpu.SMEM)] + [vmem] * 10,
        out_specs=[vmem] * 4,
        out_shape=[jax.ShapeDtypeStruct((16 * rows, width), jnp.float32) for rows in ROWS]
        + [jax.ShapeDtypeStruct(part.shape, jnp.float32)],
        compiler_params=pltpu.CompilerParams(vmem_limit_bytes=VMEM),
        cost_estimate=pl.CostEstimate(
            flops=4 * length * width * STATE, bytes_accessed=12 * MIB, transcendentals=0
        ),
    )(lengths, y, c, decay, part, z_gate, *states)


def hold(array, *others):
    anywhere = pl.BlockSpec(memory_space=pl.ANY)

    def kernel(*refs):
        pass

    return pl.pallas_call(
        kernel,
        in_specs=[anywhere] * (1 + len(others)),
        out_specs=anywhere,
        out_shape=jax.ShapeDtypeStruct(array.shape, array.dtype),
        input_output_aliases={0: 0},
        compiler_params=pltpu.CompilerParams(vmem_limit_bytes=VMEM),
        cost_estimate=pl.CostEstimate(flops=0, bytes_accessed=0, transcendentals=0),
    )(array, *others)


def choose(near, far, *others):
    rows, columns = near.shape
    tile = pl.BlockSpec((rows // 2, columns), lambda i: (i, 0))

    def kernel(near_ref, far_ref, *refs):
        core = lax.axis_index("req") & 1
        refs[-1][...] = jnp.where(core == 0, far_ref[...], near_ref[...])

    return pl.pallas_call(
        kernel,
        grid=(2,),
        in_specs=[tile] * 2 + [pl.BlockSpec(memory_space=pl.ANY)] * len(others),
        out_specs=tile,
        out_shape=jax.ShapeDtypeStruct(near.shape, near.dtype),
        compiler_params=pltpu.CompilerParams(vmem_limit_bytes=VMEM),
        cost_estimate=pl.CostEstimate(flops=0, bytes_accessed=3 * MIB, transcendentals=0),
    )(near, far, *others)


ORDER = ((2, 1, 0, 3), (2, 3, 0, 1))
TILE = 512


SENT = ((2, 1), (2, 3))
KEPT = ((3, 0), (1, 0))


def product(blocks, majors, weight, w_far, others):
    depth = weight.shape[0]
    width = weight.shape[1] // 4
    rows = blocks[0].shape[0] // 16
    lines = 4 * rows
    tiles = width // (2 * TILE)
    opening = isinstance(w_far, tuple)
    join = majors is SENT
    heights = (2 * lines, 2 * lines) if join else (lines,) * 4

    def kernel(*refs):
        own, near, opposite, far, w_own_ref = refs[:5]
        outs, own_side, far_side = refs[-2 - opening - len(heights) : -2], refs[-2], refs[-1]
        step = pl.program_id(0)

        @pl.when(step == 0)
        def _():
            at = 0
            for side, (own_ref, far_ref) in enumerate(((own, opposite), (near, far))):
                for major in majors[side]:
                    span = slice(major * lines, (major + 1) * lines)
                    own_side[at : at + lines] = own_ref[span].astype(jnp.bfloat16)
                    far_side[at : at + lines] = far_ref[span].astype(jnp.bfloat16)
                    at += lines

        if opening:
            far_weight = outs[len(heights)]

            @pl.when(step < tiles)
            def _():
                far_weight[...] = refs[5][...].astype(jnp.bfloat16)

            @pl.when(step >= tiles)
            def _():
                far_weight[...] = refs[6][...].astype(jnp.bfloat16)
        else:
            far_weight = refs[5]

        total = jnp.dot(own_side[...], w_own_ref[...], preferred_element_type=jnp.float32)
        total += jnp.dot(far_side[...], far_weight[...], preferred_element_type=jnp.float32)
        for side in range(2):
            for which in range(2):
                ref = outs[side] if join else outs[2 * side + which]
                for at, minor in enumerate(ORDER[side]):
                    to = (join * which * 4 + at) * rows
                    start = (side * 2 + which) * lines + minor * rows
                    ref[to : to + rows, :] = total[start : start + rows]

    def own_columns(i):
        _, _, hi, lo, core = place_in_mesh()
        side = jnp.where(i < tiles, core, 1 - core)
        return (0, ((2 * hi + lo) * 2 + side) * tiles + jnp.where(i < tiles, i, i - tiles))

    def tile(rows):
        return pl.BlockSpec((rows, TILE), lambda i: (0, i))

    if opening:
        extra_specs = [
            pl.BlockSpec((depth, TILE), lambda i: (0, jnp.minimum(i, tiles - 1))),
            pl.BlockSpec((depth, TILE), lambda i: (0, jnp.maximum(i - tiles, 0))),
        ]
        extra = w_far
    else:
        extra_specs = [tile(depth)]
        extra = (w_far,)
    out_specs = [tile(h) for h in heights]
    out_shape = [jax.ShapeDtypeStruct((h, width), jnp.float32) for h in heights]
    if opening:
        out_specs.append(tile(depth))
        out_shape.append(jax.ShapeDtypeStruct((depth, width), jnp.bfloat16))
    return pl.pallas_call(
        kernel,
        grid=(2 * tiles,),
        in_specs=[pl.BlockSpec(b.shape, lambda i: (0, 0)) for b in blocks]
        + [pl.BlockSpec((depth, TILE), own_columns)]
        + extra_specs
        + [pl.BlockSpec(memory_space=pl.ANY)] * len(others),
        out_specs=out_specs,
        out_shape=out_shape,
        scratch_shapes=[pltpu.VMEM((4 * lines, depth), jnp.bfloat16)] * 2,
        compiler_params=pltpu.CompilerParams(vmem_limit_bytes=VMEM),
        cost_estimate=pl.CostEstimate(
            flops=16 * lines * depth * width,
            bytes_accessed=16 * lines * depth + 4 * depth * width + 16 * lines * width,
            transcendentals=0,
        ),
    )(*blocks, weight, *extra, *others)


def relay(one_b, three_a, got1, got3, *others):
    lines, columns = one_b.shape
    tile = pl.BlockSpec((lines, columns // 2), lambda i: (0, i))

    def kernel(*refs):
        one_ref, three_ref, got1_ref, got3_ref = refs[:4]
        refs[-2][...] = one_ref[...] + got3_ref[...]
        refs[-1][...] = three_ref[...] + got1_ref[...]

    return pl.pallas_call(
        kernel,
        grid=(2,),
        in_specs=[tile] * 4 + [pl.BlockSpec(memory_space=pl.ANY)] * len(others),
        out_specs=[tile] * 2,
        out_shape=[jax.ShapeDtypeStruct((lines, columns), jnp.float32)] * 2,
        compiler_params=pltpu.CompilerParams(vmem_limit_bytes=VMEM),
        cost_estimate=pl.CostEstimate(
            flops=0, bytes_accessed=24 * lines * columns, transcendentals=0
        ),
    )(one_b, three_a, got1, got3, *others)


def combine(chunks, *others):
    operands, specs, heights = [], [], []
    for chunk in chunks:
        lines, columns = chunk[0].shape
        heights.append(lines // 4)
        for place, array in enumerate(chunk):
            operands.append(array)
            specs.append(pl.BlockSpec((lines, TILE), lambda i, at=place % 3 == 1: (int(at), i)))
    total = sum(heights)

    def kernel(*refs):
        first, third, one_b, three_a, zero_a, zero_b = refs[-6:]
        here = 0
        for chunk, rows in enumerate(heights):
            kept_a, got_a, back_a, kept_b, got_b, back_b = refs[6 * chunk : 6 * chunk + 6]
            sum_a = kept_a[...] + got_a[...] + back_a[...]
            sum_b = kept_b[...] + got_b[...] + back_b[...]
            for ref, summed, minor, start in (
                (first, sum_a, 0, here),
                (first, sum_a, 1, total + here),
                (zero_a, sum_a, 2, here),
                (three_a, sum_a, 3, here),
                (third, sum_b, 0, here),
                (third, sum_b, 1, total + here),
                (zero_b, sum_b, 2, here),
                (one_b, sum_b, 3, here),
            ):
                ref[start : start + rows] = summed[minor * rows : (minor + 1) * rows]
            here += rows

    made = (2 * total, 2 * total, total, total, total, total)
    return pl.pallas_call(
        kernel,
        grid=(columns // TILE,),
        in_specs=specs + [pl.BlockSpec(memory_space=pl.ANY)] * len(others),
        out_specs=[pl.BlockSpec((h, TILE), lambda i: (0, i)) for h in made],
        out_shape=[jax.ShapeDtypeStruct((h, columns), jnp.float32) for h in made],
        compiler_params=pltpu.CompilerParams(vmem_limit_bytes=VMEM),
        cost_estimate=pl.CostEstimate(
            flops=0, bytes_accessed=128 * total * columns, transcendentals=0
        ),
    )(*operands, *others)


def finish_kernel(*refs):
    hi = lax.axis_index("head") & 1
    outs = refs[12:]
    for side in range(2):
        for way in range(2):
            to = 0
            for part in range(2):
                kept, got, back = refs[6 * part + 3 * side : 6 * part + 3 * side + 3]
                lines = kept.shape[0]
                for block in range(lines // 16):
                    row = pl.multiple_of(block * 16 + (hi ^ way) * 8, 8)
                    later = pl.multiple_of(lines + row, 8)
                    outs[2 * way + side][to : to + 8, :] = (
                        kept[pl.ds(row, 8), :] + got[pl.ds(later, 8), :] + back[pl.ds(row, 8), :]
                    )
                    to += 8


def finish(*terms):
    columns = terms[0].shape[1]
    vmem = pl.BlockSpec(memory_space=pltpu.VMEM)
    return pl.pallas_call(
        finish_kernel,
        in_specs=[vmem] * 12,
        out_specs=[vmem] * 4,
        out_shape=[jax.ShapeDtypeStruct((32, columns), jnp.float32)] * 4,
        compiler_params=pltpu.CompilerParams(vmem_limit_bytes=VMEM),
        cost_estimate=pl.CostEstimate(flops=0, bytes_accessed=4 * MIB, transcendentals=0),
    )(*terms)


def assemble_kernel(own, near, across, far, mixed):
    _, _, hi, lo, core = place_in_mesh()
    half = own.shape[1] // 2
    for flip, source in enumerate((own, near, across, far)):
        place = (2 * hi + lo) ^ flip
        for side in range(2):
            start = pl.multiple_of((place * 2 + (side ^ core)) * half, half)
            for request in range(2):
                mixed[request, :, pl.ds(start, half)] = source[
                    request * 16 : request * 16 + 16, side * half : (side + 1) * half
                ]


def assemble(pieces):
    rows, columns = pieces[0].shape
    vmem = pl.BlockSpec(memory_space=pltpu.VMEM)
    return pl.pallas_call(
        assemble_kernel,
        in_specs=[vmem] * 4,
        out_specs=vmem,
        out_shape=jax.ShapeDtypeStruct((2, rows // 2, 4 * columns), jnp.float32),
        compiler_params=pltpu.CompilerParams(vmem_limit_bytes=VMEM),
        cost_estimate=pl.CostEstimate(flops=0, bytes_accessed=2 * MIB, transcendentals=0),
    )(*pieces)


def project(gated, out_weight, w_near):
    def ring(own):
        return (own, swap(own, lo=1), swap(own, hi=1, lo=1))

    def first_round(parts, axis):
        return (swap(parts[0], **{axis: 1}), swap(parts[1], **{axis: 3}))

    def second_round(parts, got, axis, *others):
        sent = relay(parts[2], parts[3], *got, *others)
        return (swap(sent[0], **{axis: 1}), swap(sent[1], **{axis: 3})), sent[0]

    def multiply(blocks, w_far, *others):
        sent = product(blocks, SENT, out_weight, w_far, others)
        w_far = sent[2] if isinstance(w_far, tuple) else w_far
        three_a, zero_a, one_b, zero_b = product(blocks, KEPT, out_weight, w_far, (sent[0],))
        return (sent[0], sent[1], one_b, three_a, zero_a, zero_b), w_far

    def terms(parts, got, back):
        return (parts[4], got[0], back[1], parts[5], got[1], back[0])

    own, near, far = ring(gated[0])
    chosen = choose(near, far)
    w_near = hold(w_near, chosen)
    w_far = (w_near, swap(w_near, core=1))
    opposite = cross(chosen)
    blocks = (own, near, opposite, far)
    own, near, far = ring(hold(gated[1], opposite))
    parts_0, w_far = multiply(blocks, w_far)
    got_0 = first_round(parts_0, "first")

    chosen = choose(near, far, parts_0[4])
    opposite = cross(chosen)
    blocks = (own, near, opposite, far)
    back_0, token = second_round(parts_0, got_0, "first", chosen)
    own, near, far = ring(hold(gated[2], opposite, token))
    parts_1, _ = multiply(blocks, w_far, back_0[0], back_0[1])
    got_1 = first_round(parts_1, "first")

    chosen = choose(near, far, parts_1[4])
    blocks = (own, near, cross(chosen), far)
    back_1, token = second_round(parts_1, got_1, "first", chosen)
    parts_2, _ = multiply(blocks, w_far, token)
    got_2 = first_round(parts_2, "first")

    later_a = combine([terms(parts_0, got_0, back_0), terms(parts_1, got_1, back_1)], parts_2[4])
    over_a = first_round(later_a, "second")
    back_2, token = second_round(parts_2, got_2, "first", later_a[4])
    last_a, token = second_round(later_a, over_a, "second", token)
    later_b = combine([terms(parts_2, got_2, back_2)], token)
    over_b = first_round(later_b, "second")
    last_b, _ = second_round(later_b, over_b, "second")
    kept_0, kept_1, away_0, away_1 = finish(
        *terms(later_a, over_a, last_a), *terms(later_b, over_b, last_b)
    )
    return assemble(
        (kept_0, swap(kept_1, lo=1), swap(away_0, hi=1), swap(away_1, hi=1, lo=1))
    )


def on_device(
    x_input,
    z_gate,
    bc_input,
    dt_raw,
    a_log,
    d_skip,
    conv_x,
    conv_bc,
    out_weight,
    pool_state,
    pool_xtail,
    pool_bctail,
    pool_dev,
    pool_slot,
    lengths,
):
    group = lax.axis_index("head").astype(jnp.uint32) * a_log.shape[0] >> 5
    bc_tail = pool_bctail.reshape(pool_bctail.shape[:2] + (2, GROUPS, STATE))
    bc_tail = lax.dynamic_index_in_dim(bc_tail, group, 3, keepdims=False)
    tails = jnp.concatenate([pool_xtail, bc_tail.reshape(bc_tail.shape[:2] + (2 * STATE,))], axis=-1)
    tails = jnp.pad(tails.astype(jnp.float32), ((0, 0), (5, 0), (0, 0)))
    away_0, away_1, mine, chip, tail_away, tail_mine, tail_chip, outgoing = prepare(
        pool_dev.reshape(-1), pool_slot, pool_state, tails, out_weight
    )
    w_near = swap(outgoing, hi=1, lo=1)
    tail_near = swap(tail_away, core=1)
    near_0 = swap(away_0, core=1)
    near_1 = swap(away_1, core=1)
    tail_far = swap(tail_chip + tail_near[:, 1], lo=1)
    chip = hold(chip, tail_far)
    tail_rows = tail_mine + tail_near[:, 0] + tail_far
    far_0 = swap(chip[0] + near_0[1], lo=1)
    far_1 = swap(chip[1] + near_1[1], lo=1)
    parts = scan(
        lengths, x_input, bc_input, tail_rows, conv_x, conv_bc, dt_raw, a_log, d_skip
    )
    *gated, final_state = gate(lengths, parts, z_gate, mine, near_0, near_1, far_0, far_1)
    mixed_out = project(gated, out_weight, w_near)
    return (mixed_out, final_state)


def solution(mesh):
    return jax.shard_map(
        on_device,
        mesh=mesh,
        in_specs=(
            P("req", None, "head"),
            P("req", None, "head"),
            P("req", None, None),
            P("req", "head", None),
            P("head"),
            P("head"),
            P(None, "head"),
            P(),
            P("head", None),
            P("req", "head", None),
            P("req", None, "head"),
            P("req", None, None),
            P(),
            P(),
            P("req"),
        ),
        out_specs=(P("req", "head", None), P("req", "head", None)),
        check_vma=False,
    )
```
